256 devices in a mesh: slide: 8 (over y, z_hi), tile: 32 (over x, z_lo, core).
Axes of the slice: x: 4, y: 4, z: 8 (z_hi: 2, z_lo: 4; z = z_hi * 4 + z_lo), core: 2. Of those that a mesh axis runs over, the one named last changes fastest.
Arguments:
- fine_level: bfloat16 [8, 256, 256, 256], P('slide', 'tile'), may hold values from -6 to 6
- coarse_level: bfloat16 [8, 128, 128, 256], P('slide', 'tile'), may hold values from -6 to 6
- fine_kernel: bfloat16 [256, 9, 128], replicated, may hold values from -0.125 to 0.125
- coarse_kernel: bfloat16 [256, 9, 128], replicated, may hold values from -0.125 to 0.125
- fine_gain: float32 [128], replicated, may hold values from 0.25 to 1.75
- fine_offset: float32 [128], replicated, may hold values from -3 to 3
- coarse_gain: float32 [128], replicated, may hold values from 0.25 to 1.75
- coarse_offset: float32 [128], replicated, may hold values from -3 to 3
- class_kernel: bfloat16 [8, 128], replicated
- class_offset: float32 [8], replicated, may hold values from -4 to 4
- tissue_labels: int32 [8, 256, 256], P('slide', 'tile'), may hold values from -1 to 7, as said below
Outputs:
- loss: float32 [], replicated
- head_grads: float32 [12, 128], replicated
- conv_grads: float32 [256, 2, 9, 128], P('tile')
The draws below stay inside these ranges and needn't reach their ends.
Inputs may be any that keep to these rules, and one draw needn't show every extreme that they name: `tissue_labels`: -1 marks a pixel without tissue, other values are classes.
All inputs are finite; a program needn't handle non-finite values.
Results may differ from the reference program's by a relative error of at most 0.0033.
Values may be sent and summed in bfloat16 or wider, within the bound.
No kernel may reach another device: no remote copies, remote signals or barrier semaphores. Data moves between devices by JAX's collectives and lax.ppermute only.
A program may use at most 128 MiB of HBM per device.

```python
import jax
import jax.numpy as jnp
from jax import lax

FPN_CH = 256
HEAD_CH = 128
GROUPS = 32
CLASSES = 8
COLS = 256
SLIDES = 8
ROWS = 256


def draw_class_kernel(key, part):
    first_key = jax.random.fold_in(jax.random.fold_in(key, 71), 0)
    base = jax.random.normal(first_key, (CLASSES, HEAD_CH), jnp.float32) / jnp.sqrt(jnp.float32(HEAD_CH))
    return base.astype(jnp.bfloat16)


def draw_tissue_labels(key, part):
    first_key, second_key = jax.random.split(jax.random.fold_in(key, 53))
    shape = (SLIDES, ROWS, COLS)
    draws = jax.random.randint(first_key, shape, 0, 1000, dtype=jnp.int32)
    classes = jax.random.randint(second_key, shape, 0, CLASSES, dtype=jnp.int32)
    row_index = lax.broadcasted_iota(jnp.int32, shape, 1)
    threshold = 250 + 500 * row_index // ROWS
    return jnp.where(draws < threshold, classes, -1).astype(jnp.int32)


def strengthened(result, stream_key, source, target, blocks, factor):
    def block_of(axis_at):
        return (jnp.arange(result.shape[axis_at]) // (result.shape[axis_at] // blocks)).reshape((-1,) + (1,) * (result.ndim - 1 - axis_at))

    one_side = jax.random.permutation(stream_key, blocks)[block_of(target)]
    other_side = (block_of(target) + blocks // 2) % blocks
    return jnp.where((block_of(source) == one_side) | (block_of(source) == other_side), factor * result, result)


def level_of(rng, extent, cuts, smallest, top_value):
    level = 1.0
    for axis_at, shards_of in cuts:
        steps = jax.random.uniform(jax.random.fold_in(jax.random.fold_in(rng, 6), axis_at), (shards_of,), jnp.float32, smallest / len(cuts), top_value / len(cuts))
        level = level * jnp.repeat(jnp.exp(steps), extent[axis_at] // shards_of).reshape((-1,) + (1,) * (len(extent) - 1 - axis_at))
    return level


def noise(stream_key, shape, scale, limit, cuts=(), kind=jnp.bfloat16):
    values = scale * jax.random.normal(stream_key, shape, jnp.float32)
    if cuts:
        values = values * level_of(stream_key, shape, cuts, -0.22, 0.18)
    return jnp.clip(values, -limit, limit).astype(kind)


def gaussian_with(key, extent, scale, limit, cuts, heavy, kind=jnp.bfloat16):
    entries = scale * jax.random.normal(key, extent, jnp.float32)
    if cuts:
        entries = entries * level_of(key, extent, cuts, -0.22, 0.18)
    return jnp.clip(strengthened(entries, jax.random.fold_in(key, 3), *heavy), -limit, limit).astype(kind)


def setup_inputs(seed: int = 0) -> dict:
    key_of = jax.random.split(jax.random.key(seed), 12)
    return {
        "fine_level": gaussian_with(key_of[0], (SLIDES, ROWS, COLS, FPN_CH), 1.0, 6.0, ((0, 8), (1, 32)), (1, 3, 32, 2.75)),
        "coarse_level": gaussian_with(key_of[1], (SLIDES, ROWS // 2, COLS // 2, FPN_CH), 1.0, 6.0, ((0, 8), (1, 32)), (1, 3, 32, 2.75)),
        "fine_kernel": noise(key_of[2], (FPN_CH, 9, HEAD_CH), (9 * FPN_CH) ** -0.5, 0.125),
        "coarse_kernel": noise(key_of[3], (FPN_CH, 9, HEAD_CH), (9 * FPN_CH) ** -0.5, 0.125),
        "fine_gain": jnp.clip(1.0 + 0.15 * jax.random.normal(key_of[4], (HEAD_CH,), jnp.float32), 0.25, 1.75),
        "fine_offset": noise(key_of[5], (HEAD_CH,), 0.5, 3.0, (), jnp.float32),
        "coarse_gain": jnp.clip(1.0 + 0.15 * jax.random.normal(key_of[6], (HEAD_CH,), jnp.float32), 0.25, 1.75),
        "coarse_offset": noise(key_of[7], (HEAD_CH,), 0.5, 3.0, (), jnp.float32),
        "class_kernel": draw_class_kernel(jax.random.fold_in(key_of[11], 71), 0),
        "class_offset": noise(key_of[9], (CLASSES,), 1.0, 4.0, (), jnp.float32),
        "tissue_labels": draw_tissue_labels(jax.random.fold_in(key_of[11], 71), 0),
    }


epsilon = 1e-05

def shifted(padded, height, width, position):
    row_step = position // 3
    col_step = position % 3
    return padded[row_step:row_step + height, col_step:col_step + width].reshape(height * width, -1)

def convolve(padded, kernel, height, width):
    total = jnp.zeros((height * width, kernel.shape[2]), jnp.float32)
    for position in range(9):
        total = total + jnp.dot(shifted(padded, height, width, position), kernel[:, position, :], preferred_element_type=jnp.float32)
    return total

def group_sums(values, groups):
    return values.reshape(values.shape[0], groups, -1).sum(axis=(0, 2))

def spread(per_group, channels):
    return jnp.repeat(per_group, channels // per_group.shape[0])

def kernel_grads(padded, upstream, height, width):
    taps = [lax.dot_general(shifted(padded, height, width, position), upstream, (((0,), (0,)), ((), ())), preferred_element_type=jnp.float32) for position in range(9)]
    return jnp.stack(taps, 1)

def one_slide(level_fine, level_coarse, labels, fine_kernel, coarse_kernel, fine_gain, fine_offset, coarse_gain, coarse_offset, class_kernel, class_offset, total):
    height, width = (level_fine.shape[0], level_fine.shape[1])
    channels = fine_kernel.shape[2]
    states = []
    for level, kernel, gain, offset in ((level_fine, fine_kernel, fine_gain, fine_offset), (level_coarse, coarse_kernel, coarse_gain, coarse_offset)):
        rows_here, cols_here = (level.shape[0], level.shape[1])
        padded = jnp.pad(level, ((1, 1), (1, 1), (0, 0)))
        conv_out = convolve(padded, kernel, rows_here, cols_here)
        number = rows_here * cols_here * (channels // GROUPS)
        mean = group_sums(conv_out, GROUPS) / number
        variance = group_sums(conv_out * conv_out, GROUPS) / number - mean * mean
        scale = spread(lax.rsqrt(variance + epsilon), channels)
        normed = (conv_out - spread(mean, channels)) * scale
        pre_act = normed * gain + offset
        states.append((padded, normed, scale, pre_act, gain, number, rows_here, cols_here))
    act_fine = jnp.maximum(states[0][3], 0.0).reshape(height, width, channels)
    act_coarse = jnp.maximum(states[1][3], 0.0).reshape(height // 2, width // 2, channels)
    upsampled = jnp.repeat(jnp.repeat(act_coarse, 2, 0), 2, 1)
    merged = (act_fine + upsampled).astype(jnp.bfloat16).reshape(height * width, channels)
    logits = lax.dot_general(class_kernel, merged, (((1,), (1,)), ((), ())), preferred_element_type=jnp.float32) + class_offset[:, None]
    flat_labels = labels.reshape(-1)
    tissue = (flat_labels >= 0).astype(jnp.float32)
    onehot = (flat_labels[None, :] == jnp.arange(CLASSES, dtype=jnp.int32)[:, None]).astype(jnp.float32)
    top = lax.optimization_barrier(jnp.max(logits, axis=0))
    lse = top + jnp.log(lax.optimization_barrier(jnp.sum(jnp.exp(logits - top[None, :]), axis=0)))
    loss_sum = jnp.sum((lse - lax.optimization_barrier(jnp.sum(onehot * logits, axis=0))) * tissue)
    dlogits = ((jnp.exp(logits - lse[None, :]) - onehot) * tissue[None, :] / total).astype(jnp.bfloat16)
    class_grad = jnp.dot(dlogits, merged, preferred_element_type=jnp.float32)
    dmerged = lax.dot_general(dlogits, class_kernel, (((0,), (0,)), ((), ())), preferred_element_type=jnp.float32)
    dact_fine = dmerged
    dact_coarse = dmerged.reshape(height // 2, 2, width // 2, 2, channels).sum(axis=(1, 3)).reshape(-1, channels)
    norm_rows = []
    conv_rows = []
    for state, upstream in ((states[0], dact_fine), (states[1], dact_coarse)):
        padded, normed, scale, pre_act, gain, number, rows_here, cols_here = state
        dpre = upstream * (pre_act > 0).astype(jnp.float32)
        norm_rows.append(lax.optimization_barrier(jnp.sum(dpre * normed, axis=0)))
        norm_rows.append(lax.optimization_barrier(jnp.sum(dpre, axis=0)))
        dnorm = dpre * gain
        first = spread(group_sums(dnorm, GROUPS) / number, channels)
        second = spread(group_sums(dnorm * normed, GROUPS) / number, channels)
        dconv = ((dnorm - first - normed * second) * scale).astype(jnp.bfloat16)
        conv_rows.append(kernel_grads(padded, dconv, rows_here, cols_here))
    head = jnp.concatenate([jnp.stack(norm_rows, 0), class_grad], 0)
    return (loss_sum, head, jnp.stack(conv_rows, 1))

def reference(fine_level, coarse_level, fine_kernel, coarse_kernel, fine_gain, fine_offset, coarse_gain, coarse_offset, class_kernel, class_offset, tissue_labels):
    total = jnp.sum((tissue_labels >= 0).astype(jnp.float32))

    def run(index):
        return one_slide(fine_level[index], coarse_level[index], tissue_labels[index], fine_kernel, coarse_kernel, fine_gain, fine_offset, coarse_gain, coarse_offset, class_kernel, class_offset, total)
    loss_sums, heads, convs = lax.map(run, jnp.arange(SLIDES, dtype=jnp.int32))
    return (jnp.sum(loss_sums) / total, lax.optimization_barrier(jnp.sum(heads, axis=0)), lax.optimization_barrier(jnp.sum(convs, axis=0)))
```

```python
import functools

import jax
import jax.numpy as jnp
from jax import lax
from jax.experimental import pallas as pl
from jax.experimental.pallas import tpu as pltpu
from jax.sharding import PartitionSpec as P

GROUPS = 32
epsilon = 1e-05
F32 = jnp.float32
BF16 = jnp.bfloat16
VMEM_BYTES = 48 * 1024 * 1024


def call(kernel, outs, scratch=(), **more):
    return pl.pallas_call(
        kernel,
        out_shape=outs,
        scratch_shapes=list(scratch),
        compiler_params=pltpu.CompilerParams(vmem_limit_bytes=VMEM_BYTES),
        **more,
    )


def shape(*dims, dtype=F32):
    return jax.ShapeDtypeStruct(dims, dtype)


def moved(values, step):
    count = values.shape[0]
    rows = lax.broadcasted_iota(jnp.int32, values.shape, 0)
    edge = 0 if step > 0 else count - 1
    return jnp.where(rows == edge, 0.0, pltpu.roll(values, step % count, 0))


def taps_of(kernel_ref, row_step):
    return jnp.concatenate([kernel_ref[3 * row_step + b] for b in range(3)], axis=1)


def joined(products, channels):
    left = products[:, :channels]
    middle = products[:, channels : 2 * channels]
    right = products[:, 2 * channels :]
    return moved(left, 1) + middle + moved(right, -1)


def interior_kernel(rows_fine, rows_coarse, fine_ref, coarse_ref, fk_ref, ck_ref, fconv_ref, cconv_ref):
    for x_ref, k_ref, out_ref, rows in (
        (coarse_ref, ck_ref, cconv_ref, rows_coarse),
        (fine_ref, fk_ref, fconv_ref, rows_fine),
    ):
        cols = x_ref.shape[0] // rows
        channels = k_ref.shape[2]
        for row in range(rows):
            total = None
            for a in range(3):
                source = row + a - 1
                if 0 <= source < rows:
                    part = jnp.dot(
                        x_ref[source * cols : (source + 1) * cols, :],
                        taps_of(k_ref, a),
                        preferred_element_type=F32,
                    )
                    total = part if total is None else total + part
            out_ref[row * cols : (row + 1) * cols, :] = joined(total, channels)


def edges_kernel(
    rows_fine,
    rows_coarse,
    fpart_ref,
    cpart_ref,
    above_ref,
    below_ref,
    fk_ref,
    ck_ref,
    fconv_ref,
    cconv_ref,
    stats_ref,
):
    stats_ref[...] = jnp.zeros_like(stats_ref)
    start = 0
    for level, (part_ref, k_ref, out_ref, rows) in enumerate(
        ((fpart_ref, fk_ref, fconv_ref, rows_fine), (cpart_ref, ck_ref, cconv_ref, rows_coarse))
    ):
        cols = part_ref.shape[0] // rows
        channels = k_ref.shape[2]
        first = jnp.zeros((1, channels), F32)
        second = jnp.zeros((1, channels), F32)
        for row in range(rows):
            value = part_ref[row * cols : (row + 1) * cols, :]
            for edge, halo_ref, a in ((0, above_ref, 0), (rows - 1, below_ref, 2)):
                if row == edge:
                    value = value + joined(
                        jnp.dot(
                            halo_ref[start : start + cols, :],
                            taps_of(k_ref, a),
                            preferred_element_type=F32,
                        ),
                        channels,
                    )
            out_ref[row * cols : (row + 1) * cols, :] = value
            first = first + jnp.sum(value, axis=0, keepdims=True)
            second = second + jnp.sum(value * value, axis=0, keepdims=True)
        stats_ref[2 * level : 2 * level + 1, :] = first
        stats_ref[2 * level + 1 : 2 * level + 2, :] = second
        start += cols


def turned_kernel(fine_ref, coarse_ref, above_ref, below_ref, fturn_ref, cturn_ref):
    channels = fine_ref.shape[1]
    tile = lax.axis_index("tile")
    core, z, x = tile % 2, (tile // 2) % 4, tile // 8
    row = lax.broadcasted_iota(jnp.int32, (channels, channels), 0)
    col = lax.broadcasted_iota(jnp.int32, (channels, channels), 1)
    to_core = lax.rem(core + row // 128, 2)
    to_x = lax.rem(x + lax.rem(row // 32, 4), 4)
    to_z = lax.rem(z + lax.rem(row // 8, 4), 4)
    channel = (to_x * 8 + to_z * 2 + to_core) * 8 + lax.rem(row, 8)
    order = (col == channel).astype(F32).astype(BF16)
    start = 0
    for x_ref, out_ref, cols in (
        (fine_ref, fturn_ref, above_ref.shape[0] * 2 // 3),
        (coarse_ref, cturn_ref, above_ref.shape[0] // 3),
    ):
        inner = x_ref.shape[0]
        for ref, at, size, to in (
            (above_ref, start, cols, 0),
            (x_ref, 0, inner, cols),
            (below_ref, start, cols, cols + inner),
        ):
            out_ref[:, to : to + size] = lax.dot_general(
                order, ref[at : at + size, :], (((1,), (1,)), ((), ())), preferred_element_type=F32
            ).astype(BF16)
        start += cols


def same_group(channels):
    per_group = channels // GROUPS
    row = lax.broadcasted_iota(jnp.int32, (channels, channels), 0)
    col = lax.broadcasted_iota(jnp.int32, (channels, channels), 1)
    return (row // per_group == col // per_group).astype(F32)


def over_group(rows, members):
    return jnp.dot(rows, members, precision=lax.Precision.HIGHEST, preferred_element_type=F32)


def norm_terms(sums, level, number):
    mean = sums[2 * level : 2 * level + 1, :] / number
    variance = sums[2 * level + 1 : 2 * level + 2, :] / number - mean * mean
    return mean, lax.rsqrt(variance + epsilon)


def loss_kernel(
    rows_fine,
    numbers,
    fconv_ref,
    cconv_ref,
    stats_ref,
    fgain_ref,
    foffset_ref,
    cgain_ref,
    coffset_ref,
    class_ref,
    bias_ref,
    labels_ref,
    fdpre_ref,
    cdpre_ref,
    head_ref,
    wide_ref,
    sum_ref,
):
    channels = fconv_ref.shape[1]
    cols = fconv_ref.shape[0] // rows_fine
    half = cols // 2
    classes = class_ref.shape[0]
    sums = over_group(stats_ref[...], same_group(channels))
    fmean, fscale = norm_terms(sums, 0, numbers[0])
    cmean, cscale = norm_terms(sums, 1, numbers[1])
    weights = class_ref[...]
    bias = bias_ref[...]
    rows_sum = [jnp.zeros((1, channels), F32) for _ in range(4)]
    class_sum = jnp.zeros((classes, channels), F32)
    loss_sum = jnp.zeros((1, cols), F32)
    tissue_sum = jnp.zeros((1, cols), F32)
    class_id = lax.broadcasted_iota(jnp.int32, (classes, cols), 0)
    for pair in range(rows_fine // 2):
        cnormed = (cconv_ref[pair * half : (pair + 1) * half, :] - cmean) * cscale
        cpre = cnormed * cgain_ref[...] + coffset_ref[...]
        cact = jnp.maximum(cpre, 0.0)
        wide_ref[pl.ds(0, half, stride=2), :] = cact
        wide_ref[pl.ds(1, half, stride=2), :] = cact
        up = wide_ref[...]
        both = None
        for row in (2 * pair, 2 * pair + 1):
            here = slice(row * cols, (row + 1) * cols)
            normed = (fconv_ref[here, :] - fmean) * fscale
            pre = normed * fgain_ref[...] + foffset_ref[...]
            merged = (jnp.maximum(pre, 0.0) + up).astype(BF16)
            logits = (
                lax.dot_general(
                    weights, merged, (((1,), (1,)), ((), ())), preferred_element_type=F32
                )
                + bias
            )
            top = jnp.max(logits, axis=0, keepdims=True)
            lse = top + jnp.log(jnp.sum(jnp.exp(logits - top), axis=0, keepdims=True))
            label = labels_ref[row : row + 1, :]
            tissue = (label >= 0).astype(F32)
            onehot = (label == class_id).astype(F32)
            loss_sum = loss_sum + (lse - jnp.sum(onehot * logits, axis=0, keepdims=True)) * tissue
            tissue_sum = tissue_sum + tissue
            dlogits = (jnp.exp(logits - lse) - onehot) * tissue
            class_sum = class_sum + jnp.dot(
                dlogits.astype(BF16), merged, preferred_element_type=F32
            )
            dmerged = lax.dot_general(
                dlogits.astype(BF16), weights, (((0,), (0,)), ((), ())), preferred_element_type=F32
            )
            dpre = jnp.where(pre > 0, dmerged, 0.0)
            fdpre_ref[here, :] = dpre
            rows_sum[0] = rows_sum[0] + jnp.sum(dpre * normed, axis=0, keepdims=True)
            rows_sum[1] = rows_sum[1] + jnp.sum(dpre, axis=0, keepdims=True)
            both = dmerged if both is None else both + dmerged
        sum_ref[...] = both
        dact = sum_ref[pl.ds(0, half, stride=2), :] + sum_ref[pl.ds(1, half, stride=2), :]
        dpre = jnp.where(cpre > 0, dact, 0.0)
        cdpre_ref[pair * half : (pair + 1) * half, :] = dpre
        rows_sum[2] = rows_sum[2] + jnp.sum(dpre * cnormed, axis=0, keepdims=True)
        rows_sum[3] = rows_sum[3] + jnp.sum(dpre, axis=0, keepdims=True)
    head_ref[...] = jnp.zeros_like(head_ref)
    for at in range(4):
        head_ref[at : at + 1, :] = rows_sum[at]
    head_ref[4 : 4 + classes, :] = class_sum
    lane = lax.broadcasted_iota(jnp.int32, (1, channels), 1)
    loss_all = jnp.sum(loss_sum, axis=1, keepdims=True)
    tissue_all = jnp.sum(tissue_sum, axis=1, keepdims=True)
    head_ref[4 + classes : 5 + classes, :] = jnp.where(
        lane == 0, loss_all, jnp.where(lane == 1, tissue_all, 0.0)
    )


def weights_kernel(
    rows_fine,
    numbers,
    fconv_ref,
    cconv_ref,
    fdpre_ref,
    cdpre_ref,
    stats_ref,
    back_ref,
    fgain_ref,
    cgain_ref,
    fturn_ref,
    cturn_ref,
    keep_ref,
    send_ref,
    fd_ref,
    cd_ref,
):
    channels = fconv_ref.shape[1]
    members = same_group(channels)
    sums = over_group(stats_ref[...], members)
    kept = keep_ref.shape[0] // 16
    for level, (conv_ref, dpre_ref, gain_ref, turn_ref, d_ref, rows) in enumerate(
        (
            (fconv_ref, fdpre_ref, fgain_ref, fturn_ref, fd_ref, rows_fine),
            (cconv_ref, cdpre_ref, cgain_ref, cturn_ref, cd_ref, rows_fine // 2),
        )
    ):
        cols = conv_ref.shape[0] // rows
        mean, scale = norm_terms(sums, level, numbers[level])
        gain = gain_ref[...]
        means = over_group(back_ref[2 * level : 2 * level + 2, :] * gain, members) / numbers[level]
        with_normed, plain = means[0:1, :], means[1:2, :]
        for row in range(rows):
            here = slice(row * cols, (row + 1) * cols)
            normed = (conv_ref[here, :] - mean) * scale
            dconv = (dpre_ref[here, :] * gain - plain - normed * with_normed) * scale
            d_ref[here, :channels] = moved(dconv, -1).astype(BF16)
            d_ref[here, channels : 2 * channels] = dconv.astype(BF16)
            d_ref[here, 2 * channels :] = moved(dconv, 1).astype(BF16)
        for a in range(3):
            product = jnp.dot(
                turn_ref[:, a * cols : a * cols + rows * cols], d_ref[...], preferred_element_type=F32
            )
            wide = product.shape[1]
            span = slice(a * wide, (a + 1) * wide)
            for block in range(product.shape[0] // 8):
                piece = product[8 * block : 8 * block + 8, :]
                at = 16 * (block % kept) + 8 * level
                if block < kept:
                    keep_ref[at : at + 8, span] = piece
                else:
                    send_ref[at : at + 8, span] = piece


def first_sum_kernel(keep_ref, sent_ref, own_ref, *out_refs):
    size = own_ref.shape[0]
    own_ref[...] = keep_ref[:size, :] + sent_ref[:size, :].astype(F32)
    for at, out_ref in enumerate(out_refs):
        here = slice((at + 1) * size, (at + 2) * size)
        out_ref[...] = (keep_ref[here, :] + sent_ref[here, :].astype(F32)).astype(BF16)


def next_sum_kernel(keep_ref, one_ref, two_ref, three_ref, own_ref, *out_refs):
    size = own_ref.shape[0]
    for at, out_ref in enumerate((own_ref, *out_refs)):
        here = slice(at * size, (at + 1) * size)
        out_ref[...] = (
            (keep_ref[here, :] + one_ref[here, :].astype(F32))
            + (two_ref[here, :].astype(F32) + three_ref[here, :].astype(F32))
        ).astype(out_ref.dtype)


def last_tile_kernel(keep_ref, one_ref, two_ref, three_ref, head_ref, out_ref):
    wide = keep_ref.shape[1]
    out_ref[:, :wide] = (keep_ref[...] + one_ref[...].astype(F32)) + (
        two_ref[...].astype(F32) + three_ref[...].astype(F32)
    )
    out_ref[:, wide:] = head_ref[...]


def final_kernel(own_ref, one_ref, two_ref, three_ref, loss_ref, head_ref, grads_ref):
    whole = (own_ref[...] + two_ref[...]) + (one_ref[...] + three_ref[...])
    rows = head_ref.shape[0]
    channels = head_ref.shape[1]
    wide = whole.shape[1] - channels
    head = whole[:, wide:]
    total = head[rows : rows + 1, 1:2]
    loss_ref[...] = head[rows : rows + 1, 0:1] / total
    head_ref[...] = head[:rows, :] / total
    taps = wide // channels
    for level in range(2):
        for tap in range(taps):
            grads_ref[pl.ds(2 * tap + level, 8, stride=2 * taps), :] = (
                whole[8 * level : 8 * level + 8, tap * channels : (tap + 1) * channels] / total
            )


def core_pairs():
    return [(i, i ^ 1) for i in range(32)]


def x_pairs(step):
    return [(i, (i // 8 + step) % 4 * 8 + i % 8) for i in range(32)]


def z_pairs(step):
    return [(i, i // 8 * 8 + (i // 2 + step) % 4 * 2 + i % 2) for i in range(32)]


def tile_sum(values):
    values = values + lax.ppermute(values, "tile", core_pairs())
    for pairs in (x_pairs, z_pairs):
        one, two, three = [lax.ppermute(values, "tile", pairs(step)) for step in (1, 2, 3)]
        values = (values + two) + (one + three)
    return values


def per_device(
    fine_level,
    coarse_level,
    fine_kernel,
    coarse_kernel,
    fine_gain,
    fine_offset,
    coarse_gain,
    coarse_offset,
    class_kernel,
    class_offset,
    tissue_labels,
):
    tiles = lax.axis_size("tile")
    in_channels, _, channels = fine_kernel.shape
    _, height, width, _ = fine_level.shape
    classes = class_kernel.shape[0]
    numbers = (
        float(height * tiles * width * (channels // GROUPS)),
        float(height * tiles * width * (channels // GROUPS) // 4),
    )
    fine_size, coarse_size = height * width, height * width // 4
    fine = fine_level.reshape(fine_size, in_channels)
    coarse = coarse_level.reshape(coarse_size, in_channels)
    fk = fine_kernel.transpose(1, 0, 2)
    ck = coarse_kernel.transpose(1, 0, 2)
    fgain, foffset = fine_gain[None, :], fine_offset[None, :]
    cgain, coffset = coarse_gain[None, :], coarse_offset[None, :]
    labels = tissue_labels[0]

    with jax.named_scope("halo"):
        down = jnp.concatenate([fine[-width:], coarse[-(width // 2) :]], 0)
        up = jnp.concatenate([fine[:width], coarse[: width // 2]], 0)
        above = lax.ppermute(down, "tile", [(i, i + 1) for i in range(tiles - 1)])
        below = lax.ppermute(up, "tile", [(i + 1, i) for i in range(tiles - 1)])
    with jax.named_scope("forward"):
        fpart, cpart = call(
            functools.partial(interior_kernel, height, height // 2),
            (shape(fine_size, channels), shape(coarse_size, channels)),
        )(fine, coarse, fk, ck)
        fconv, cconv, stats = call(
            functools.partial(edges_kernel, height, height // 2),
            (shape(fine_size, channels), shape(coarse_size, channels), shape(8, channels)),
        )(fpart, cpart, above, below, fk, ck)
    with jax.named_scope("turned"):
        fturn, cturn = call(
            turned_kernel,
            (
                shape(in_channels, fine_size + 2 * width, dtype=BF16),
                shape(in_channels, coarse_size + width, dtype=BF16),
            ),
        )(fine, coarse, above, below)
    with jax.named_scope("forward_sums"):
        stats = tile_sum(stats)
    with jax.named_scope("loss_and_head"):
        fdpre, cdpre, head = call(
            functools.partial(loss_kernel, height, numbers),
            (shape(fine_size, channels), shape(coarse_size, channels), shape(16, channels)),
            (pltpu.VMEM((width, channels), F32), pltpu.VMEM((width, channels), F32)),
        )(
            fconv,
            cconv,
            stats,
            fgain,
            foffset,
            cgain,
            coffset,
            class_kernel,
            class_offset[:, None],
            labels,
        )
    with jax.named_scope("backward_sums"):
        head = tile_sum(head)
    with jax.named_scope("weight_grads"):
        wide = 9 * channels
        keep, send = call(
            functools.partial(weights_kernel, height, numbers),
            (shape(in_channels, wide), shape(in_channels, wide)),
            (
                pltpu.VMEM((fine_size, 3 * channels), BF16),
                pltpu.VMEM((coarse_size, 3 * channels), BF16),
            ),
        )(fconv, cconv, fdpre, cdpre, stats, head, fgain, cgain, fturn, cturn)
    with jax.named_scope("over_tiles"):
        sent = lax.ppermute(send.astype(BF16), "tile", core_pairs())
        size = in_channels // 4
        parts = call(
            first_sum_kernel, (shape(size, wide),) + (shape(size, wide, dtype=BF16),) * 3
        )(keep, sent)
        got = [lax.ppermute(parts[step], "tile", x_pairs(step)) for step in (1, 2, 3)]
        size = size // 4
        parts = call(
            next_sum_kernel, (shape(size, wide),) + (shape(size, wide, dtype=BF16),) * 3
        )(parts[0], *got)
        got = [lax.ppermute(parts[step], "tile", z_pairs(step)) for step in (1, 2, 3)]
        own = call(last_tile_kernel, shape(size, wide + channels))(parts[0], *got, head)
    with jax.named_scope("over_slides"):
        slides = lax.axis_size("slide")
        own = own + lax.ppermute(own, "slide", [(i, i ^ 1) for i in range(slides)])
        got = [
            lax.ppermute(own, "slide", [(i, (i + 2 * step) % slides) for i in range(slides)])
            for step in (1, 2, 3)
        ]
        loss, head_grads, grads = call(
            final_kernel,
            (shape(1, 1), shape(4 + classes, channels), shape(in_channels // tiles * 18, channels)),
        )(own, *got)
    conv_grads = grads.reshape(in_channels // tiles, 9, 2, channels).transpose(0, 2, 1, 3)
    return (loss.reshape(()), head_grads, conv_grads)


def solution(mesh):
    return jax.shard_map(
        per_device,
        mesh=mesh,
        in_specs=(
            P("slide", "tile", None, None),
            P("slide", "tile", None, None),
            P(),
            P(),
            P(),
            P(),
            P(),
            P(),
            P(),
            P(),
            P("slide", "tile", None),
        ),
        out_specs=(P(), P(), P("tile", None, None, None)),
        check_vma=False,
    )
```

```python
import functools

import jax
import jax.numpy as jnp
from jax import lax
from jax.experimental import pallas as pl
from jax.experimental.pallas import tpu as pltpu
from jax.sharding import PartitionSpec as P

GROUPS = 32
epsilon = 1e-05
F32 = jnp.float32
BF16 = jnp.bfloat16
VMEM_BYTES = 24 * 1024 * 1024


def call(kernel, outs, scratch=(), **more):
    return pl.pallas_call(
        kernel,
        out_shape=outs,
        scratch_shapes=list(scratch),
        compiler_params=pltpu.CompilerParams(vmem_limit_bytes=VMEM_BYTES),
        **more,
    )


def shape(*dims, dtype=F32):
    return jax.ShapeDtypeStruct(dims, dtype)


def moved(values, step):
    count = values.shape[0]
    rows = lax.broadcasted_iota(jnp.int32, values.shape, 0)
    edge = 0 if step > 0 else count - 1
    return jnp.where(rows == edge, 0.0, pltpu.roll(values, step % count, 0))


def taps_of(kernel_ref, row_step):
    return jnp.concatenate([kernel_ref[3 * row_step + b] for b in range(3)], axis=1)


def joined(products, channels):
    left = products[:, :channels]
    middle = products[:, channels : 2 * channels]
    right = products[:, 2 * channels :]
    return moved(left, 1) + middle + moved(right, -1)


def ends_kernel(fine_ref, coarse_ref, first_ref, last_ref, sems):
    wide = first_ref.shape[0] * 2 // 3
    half = first_ref.shape[0] // 3
    fine_end, coarse_end = fine_ref.shape[0] - wide, coarse_ref.shape[0] - half
    copies = [
        pltpu.make_async_copy(source, target, sems.at[at])
        for at, (source, target) in enumerate(
            (
                (fine_ref.at[pl.ds(fine_end, wide)], last_ref.at[pl.ds(0, wide)]),
                (fine_ref.at[pl.ds(0, wide)], first_ref.at[pl.ds(0, wide)]),
                (coarse_ref.at[pl.ds(coarse_end, half)], last_ref.at[pl.ds(wide, half)]),
                (coarse_ref.at[pl.ds(0, half)], first_ref.at[pl.ds(wide, half)]),
            )
        )
    ]
    for copy in copies:
        copy.start()
    for copy in copies:
        copy.wait()


def levels(ref, size, axis=0):
    rest = ref.shape[axis] - size
    parts = (pl.ds(0, size), pl.ds(size, rest))
    return [ref.at[part] if axis == 0 else ref.at[:, part] for part in parts]


def channel_order(channels):
    tile = lax.axis_index("tile")
    core, z, x = tile % 2, (tile // 2) % 4, tile // 8
    row = lax.broadcasted_iota(jnp.int32, (channels, channels), 0)
    col = lax.broadcasted_iota(jnp.int32, (channels, channels), 1)
    to_core = lax.rem(core + row // 128, 2)
    to_x = lax.rem(x + lax.rem(row // 32, 4), 4)
    to_z = lax.rem(z + lax.rem(row // 8, 4), 4)
    channel = (to_x * 8 + to_z * 2 + to_core) * 8 + lax.rem(row, 8)
    return (col == channel).astype(F32).astype(BF16)


def turn(order, pixels):
    return lax.dot_general(
        order, pixels, (((1,), (1,)), ((), ())), preferred_element_type=F32
    ).astype(BF16)


def interior_kernel(
    rows_fine,
    rows_coarse,
    fine_ref,
    coarse_ref,
    fk_ref,
    ck_ref,
    fgain_ref,
    foffset_ref,
    cgain_ref,
    coffset_ref,
    bias_ref,
    conv_ref,
    turn_ref,
    vectors_ref,
):
    for at, ref in enumerate((fgain_ref, foffset_ref, cgain_ref, coffset_ref)):
        vectors_ref[at : at + 1, :] = ref[...]
        vectors_ref[4 + at : 5 + at, :] = ref[...]
    for at in range(bias_ref.shape[0]):
        vectors_ref[8 + at : 9 + at, :] = jnp.full((1, vectors_ref.shape[1]), bias_ref[at], F32)
    fine_size = fine_ref.shape[0]
    fconv_ref, cconv_ref = levels(conv_ref, fine_size)
    fturn_ref, cturn_ref = levels(turn_ref, fine_size, 1)
    level_products(coarse_ref, ck_ref, cconv_ref, rows_coarse)
    level_products(fine_ref, fk_ref, fconv_ref, rows_fine)
    order = channel_order(fine_ref.shape[1])
    cturn_ref[...] = turn(order, coarse_ref[...])
    fturn_ref[...] = turn(order, fine_ref[...])


def level_products(x_ref, k_ref, out_ref, rows):
    cols = x_ref.shape[0] // rows
    channels = k_ref.shape[2]
    for row in range(rows):
        total = None
        for a in range(3):
            source = row + a - 1
            if 0 <= source < rows:
                part = jnp.dot(
                    x_ref[source * cols : (source + 1) * cols, :],
                    taps_of(k_ref, a),
                    preferred_element_type=F32,
                )
                total = part if total is None else total + part
        out_ref[row * cols : (row + 1) * cols, :] = joined(total, channels)


def edges_kernel(
    rows_fine,
    rows_coarse,
    part_ref,
    above_ref,
    below_ref,
    fk_ref,
    ck_ref,
    conv_ref,
    stats_ref,
):
    fine_size = part_ref.shape[0] * 4 // 5
    fpart_ref, cpart_ref = levels(part_ref, fine_size)
    fconv_ref, cconv_ref = levels(conv_ref, fine_size)
    start = 0
    found = []
    for part_ref, k_ref, out_ref, rows in (
        (fpart_ref, fk_ref, fconv_ref, rows_fine),
        (cpart_ref, ck_ref, cconv_ref, rows_coarse),
    ):
        cols = part_ref.shape[0] // rows
        channels = k_ref.shape[2]
        first = jnp.zeros((1, channels), F32)
        second = jnp.zeros((1, channels), F32)
        for row in range(rows):
            value = part_ref[row * cols : (row + 1) * cols, :]
            for edge, halo_ref, a in ((0, above_ref, 0), (rows - 1, below_ref, 2)):
                if row == edge:
                    value = value + joined(
                        jnp.dot(
                            halo_ref[start : start + cols, :],
                            taps_of(k_ref, a),
                            preferred_element_type=F32,
                        ),
                        channels,
                    )
            out_ref[row * cols : (row + 1) * cols, :] = value
            first = first + jnp.sum(value, axis=0, keepdims=True)
            second = second + jnp.sum(value * value, axis=0, keepdims=True)
        found += [first, second]
        start += cols
    found = jnp.concatenate(found + [jnp.zeros_like(found[0])] * 4, axis=0)
    for tile in range(stats_ref.shape[0] // 8):
        stats_ref[8 * tile : 8 * tile + 8, :] = found


def same_group(channels):
    per_group = channels // GROUPS
    row = lax.broadcasted_iota(jnp.int32, (channels, channels), 0)
    col = lax.broadcasted_iota(jnp.int32, (channels, channels), 1)
    return (row // per_group == col // per_group).astype(F32)


def over_tiles(all_ref, count):
    return jnp.sum(all_ref[...].reshape(-1, count, all_ref.shape[1]), axis=0)


def over_group(rows, members):
    return jnp.dot(rows, members, precision=lax.Precision.HIGHEST, preferred_element_type=F32)


def norm_terms(sums, level, number):
    mean = sums[2 * level : 2 * level + 1, :] / number
    variance = sums[2 * level + 1 : 2 * level + 2, :] / number - mean * mean
    return mean, lax.rsqrt(variance + epsilon)


def loss_kernel(
    rows_fine,
    numbers,
    conv_ref,
    stats_ref,
    vectors_ref,
    class_ref,
    labels_ref,
    dpre_ref,
    head_ref,
    wide_ref,
    sum_ref,
):
    fine_size = conv_ref.shape[0] * 4 // 5
    fconv_ref, cconv_ref = levels(conv_ref, fine_size)
    fdpre_ref, cdpre_ref = levels(dpre_ref, fine_size)
    channels = conv_ref.shape[1]
    cols = fconv_ref.shape[0] // rows_fine
    half = cols // 2
    classes = class_ref.shape[0]
    sums = over_group(over_tiles(stats_ref, 8), same_group(channels))
    fmean, fscale = norm_terms(sums, 0, numbers[0])
    cmean, cscale = norm_terms(sums, 1, numbers[1])
    weights = class_ref[...]
    bias = vectors_ref[8 : 8 + classes, 0:1]
    fgain, foffset = vectors_ref[0:1, :], vectors_ref[1:2, :]
    cgain, coffset = vectors_ref[2:3, :], vectors_ref[3:4, :]
    twice = jnp.concatenate([weights.astype(F32)] * 2, axis=0).astype(BF16)
    rows_sum = [jnp.zeros((1, channels), F32) for _ in range(4)]
    class_sum = jnp.zeros((classes, channels), F32)
    loss_sum = jnp.zeros((1, cols), F32)
    tissue_sum = jnp.zeros((1, cols), F32)
    class_id = lax.broadcasted_iota(jnp.int32, (classes, cols), 0)
    for pair in range(rows_fine // 2):
        cnormed = (cconv_ref[pair * half : (pair + 1) * half, :] - cmean) * cscale
        cpre = cnormed * cgain + coffset
        cact = jnp.maximum(cpre, 0.0)
        wide_ref[pl.ds(0, half, stride=2), :] = cact
        wide_ref[pl.ds(1, half, stride=2), :] = cact
        up = wide_ref[...]
        both = None
        for row in (2 * pair, 2 * pair + 1):
            here = slice(row * cols, (row + 1) * cols)
            normed = (fconv_ref[here, :] - fmean) * fscale
            pre = normed * fgain + foffset
            merged = (jnp.maximum(pre, 0.0) + up).astype(BF16)
            logits = (
                lax.dot_general(
                    weights, merged, (((1,), (1,)), ((), ())), preferred_element_type=F32
                )
                + bias
            )
            top = jnp.max(logits, axis=0, keepdims=True)
            lse = top + jnp.log(jnp.sum(jnp.exp(logits - top), axis=0, keepdims=True))
            label = labels_ref[row : row + 1, :]
            tissue = (label >= 0).astype(F32)
            onehot = (label == class_id).astype(F32)
            loss_sum = loss_sum + (lse - jnp.sum(onehot * logits, axis=0, keepdims=True)) * tissue
            tissue_sum = tissue_sum + tissue
            dlogits = (jnp.exp(logits - lse) - onehot) * tissue
            high = dlogits.astype(BF16).astype(F32)
            parts = jnp.concatenate([high, dlogits - high], axis=0).astype(BF16)
            class_part = jnp.dot(parts, merged, preferred_element_type=F32)
            class_sum = class_sum + (class_part[:classes] + class_part[classes:])
            dmerged = lax.dot_general(
                parts, twice, (((0,), (0,)), ((), ())), preferred_element_type=F32
            )
            dpre = jnp.where(pre > 0, dmerged, 0.0)
            fdpre_ref[here, :] = dpre
            rows_sum[0] = rows_sum[0] + jnp.sum(dpre * normed, axis=0, keepdims=True)
            rows_sum[1] = rows_sum[1] + jnp.sum(dpre, axis=0, keepdims=True)
            both = dmerged if both is None else both + dmerged
        sum_ref[...] = both
        dact = sum_ref[pl.ds(0, half, stride=2), :] + sum_ref[pl.ds(1, half, stride=2), :]
        dpre = jnp.where(cpre > 0, dact, 0.0)
        cdpre_ref[pair * half : (pair + 1) * half, :] = dpre
        rows_sum[2] = rows_sum[2] + jnp.sum(dpre * cnormed, axis=0, keepdims=True)
        rows_sum[3] = rows_sum[3] + jnp.sum(dpre, axis=0, keepdims=True)
    lane = lax.broadcasted_iota(jnp.int32, (1, channels), 1)
    loss_all = jnp.sum(loss_sum, axis=1, keepdims=True)
    tissue_all = jnp.sum(tissue_sum, axis=1, keepdims=True)
    counts = jnp.where(lane == 0, loss_all, jnp.where(lane == 1, tissue_all, 0.0))
    blank = jnp.zeros((11 - classes, channels), F32)
    head = jnp.concatenate(rows_sum + [class_sum, counts, blank], axis=0)
    for tile in range(head_ref.shape[0] // 16):
        head_ref[16 * tile : 16 * tile + 16, :] = head


def weights_kernel(
    rows_fine,
    numbers,
    all_conv_ref,
    all_dpre_ref,
    stats_ref,
    back_ref,
    vectors_ref,
    all_turn_ref,
    above_ref,
    below_ref,
    keep_ref,
    send_ref,
    head_ref,
    fd_ref,
    cd_ref,
    wide_ref,
):
    fine_size = fd_ref.shape[0]
    fconv_ref, cconv_ref = levels(all_conv_ref, fine_size)
    fdpre_ref, cdpre_ref = levels(all_dpre_ref, fine_size)
    fturn_ref, cturn_ref = levels(all_turn_ref, fine_size, 1)
    channels = all_conv_ref.shape[1]
    members = same_group(channels)
    sums = over_group(over_tiles(stats_ref, 8), members)
    back = over_tiles(back_ref, 16)
    head_ref[...] = back
    kept = keep_ref.shape[0] // 16
    order = channel_order(above_ref.shape[1])
    above, below = turn(order, above_ref[...]), turn(order, below_ref[...])
    start = 0
    for level, (conv_ref, dpre_ref, turn_ref, d_ref, rows) in enumerate(
        (
            (fconv_ref, fdpre_ref, fturn_ref, fd_ref, rows_fine),
            (cconv_ref, cdpre_ref, cturn_ref, cd_ref, rows_fine // 2),
        )
    ):
        size = conv_ref.shape[0]
        cols = size // rows
        mean, scale = norm_terms(sums, level, numbers[level])
        gain = vectors_ref[2 * level : 2 * level + 1, :]
        means = over_group(back[2 * level : 2 * level + 2, :] * gain, members) / numbers[level]
        with_normed, plain = means[0:1, :], means[1:2, :]
        for row in range(rows):
            here = slice(row * cols, (row + 1) * cols)
            normed = (conv_ref[here, :] - mean) * scale
            dconv = (dpre_ref[here, :] * gain - plain - normed * with_normed) * scale
            d_ref[here, :channels] = moved(dconv, -1).astype(BF16)
            d_ref[here, channels : 2 * channels] = dconv.astype(BF16)
            d_ref[here, 2 * channels :] = moved(dconv, 1).astype(BF16)
        for a in range(3):
            if a == 0:
                product = jnp.dot(
                    turn_ref[:, : size - cols], d_ref[cols:, :], preferred_element_type=F32
                ) + jnp.dot(
                    above[:, start : start + cols], d_ref[:cols, :], preferred_element_type=F32
                )
            elif a == 1:
                product = jnp.dot(turn_ref[...], d_ref[...], preferred_element_type=F32)
            else:
                product = jnp.dot(
                    turn_ref[:, cols:], d_ref[: size - cols, :], preferred_element_type=F32
                ) + jnp.dot(
                    below[:, start : start + cols],
                    d_ref[size - cols :, :],
                    preferred_element_type=F32,
                )
            wide = product.shape[1]
            span = slice(a * wide, (a + 1) * wide)
            for block in range(product.shape[0] // 8):
                piece = product[8 * block : 8 * block + 8, :]
                at = 16 * (block % kept) + 8 * level
                to_ref = keep_ref if block < kept else wide_ref
                to_ref[at : at + 8, span] = piece
        start += cols
    send_ref[...] = wide_ref[...].astype(BF16)


def first_sum_kernel(keep_ref, sent_ref, own_ref, *out_refs):
    size = own_ref.shape[0]
    own_ref[...] = keep_ref[:size, :] + sent_ref[:size, :].astype(F32)
    for at, out_ref in enumerate(out_refs):
        here = slice((at + 1) * size, (at + 2) * size)
        out_ref[...] = (keep_ref[here, :] + sent_ref[here, :].astype(F32)).astype(BF16)


def next_sum_kernel(keep_ref, one_ref, two_ref, three_ref, own_ref, *out_refs):
    size = own_ref.shape[0]
    for at, out_ref in enumerate((own_ref, *out_refs)):
        here = slice(at * size, (at + 1) * size)
        out_ref[...] = (
            (keep_ref[here, :] + one_ref[here, :].astype(F32))
            + (two_ref[here, :].astype(F32) + three_ref[here, :].astype(F32))
        ).astype(out_ref.dtype)


def last_tile_kernel(keep_ref, one_ref, two_ref, three_ref, head_ref, out_ref):
    wide = keep_ref.shape[1]
    out_ref[:, :wide] = (keep_ref[...] + one_ref[...].astype(F32)) + (
        two_ref[...].astype(F32) + three_ref[...].astype(F32)
    )
    out_ref[:, wide:] = head_ref[...]


def final_kernel(own_ref, one_ref, two_ref, three_ref, loss_ref, head_ref, grads_ref):
    whole = (own_ref[...] + two_ref[...]) + (one_ref[...] + three_ref[...])
    rows = head_ref.shape[0]
    channels = head_ref.shape[1]
    wide = whole.shape[1] - channels
    head = whole[:, wide:]
    total = head[rows : rows + 1, 1:2]
    loss_ref[...] = head[rows : rows + 1, 0:1] / total
    head_ref[...] = head[:rows, :] / total
    taps = wide // channels
    for level in range(2):
        for tap in range(taps):
            grads_ref[pl.ds(2 * tap + level, 8, stride=2 * taps), :] = (
                whole[8 * level : 8 * level + 8, tap * channels : (tap + 1) * channels] / total
            )


def core_pairs():
    return [(i, i ^ 1) for i in range(32)]


def x_pairs(step):
    return [(i, (i // 8 + step) % 4 * 8 + i % 8) for i in range(32)]


def z_pairs(step):
    return [(i, i // 8 * 8 + (i // 2 + step) % 4 * 2 + i % 2) for i in range(32)]


def per_device(
    fine_level,
    coarse_level,
    fine_kernel,
    coarse_kernel,
    fine_gain,
    fine_offset,
    coarse_gain,
    coarse_offset,
    class_kernel,
    class_offset,
    tissue_labels,
):
    tiles = lax.axis_size("tile")
    in_channels, _, channels = fine_kernel.shape
    _, height, width, _ = fine_level.shape
    classes = class_kernel.shape[0]
    numbers = (
        float(height * tiles * width * (channels // GROUPS)),
        float(height * tiles * width * (channels // GROUPS) // 4),
    )
    fine_size, coarse_size = height * width, height * width // 4
    pixels = fine_size + coarse_size
    fine = fine_level.reshape(fine_size, in_channels)
    coarse = coarse_level.reshape(coarse_size, in_channels)
    fk = fine_kernel.transpose(1, 0, 2)
    ck = coarse_kernel.transpose(1, 0, 2)
    labels = tissue_labels[0]
    vectors = [fine_gain, fine_offset, coarse_gain, coarse_offset]
    vectors = [vector[None, :] for vector in vectors]

    with jax.named_scope("halo"):
        ends = shape(width + width // 2, in_channels, dtype=BF16)
        up, down = call(
            ends_kernel,
            (ends, ends),
            (pltpu.SemaphoreType.DMA((4,)),),
            in_specs=[pl.BlockSpec(memory_space=pltpu.HBM)] * 2,
        )(fine, coarse)
        above = lax.ppermute(down, "tile", [(i, i + 1) for i in range(tiles - 1)])
        below = lax.ppermute(up, "tile", [(i + 1, i) for i in range(tiles - 1)])
    with jax.named_scope("forward"):
        whole = pl.BlockSpec(memory_space=pltpu.VMEM)
        part, turned, vectors = call(
            functools.partial(interior_kernel, height, height // 2),
            (
                shape(pixels, channels),
                shape(in_channels, pixels, dtype=BF16),
                shape(8 + classes, channels),
            ),
            in_specs=[whole] * 8 + [pl.BlockSpec(memory_space=pltpu.SMEM)],
        )(fine, coarse, fk, ck, *vectors, class_offset)
        conv, stats = call(
            functools.partial(edges_kernel, height, height // 2),
            (shape(pixels, channels), shape(8 * tiles, channels)),
            input_output_aliases={0: 0},
        )(part, above, below, fk, ck)
    with jax.named_scope("forward_sums"):
        stats = lax.all_to_all(stats, "tile", 0, 0, tiled=True)
    with jax.named_scope("loss_and_head"):
        dpre, head = call(
            functools.partial(loss_kernel, height, numbers),
            (shape(pixels, channels), shape(16 * tiles, channels)),
            (pltpu.VMEM((width, channels), F32), pltpu.VMEM((width, channels), F32)),
        )(conv, stats, vectors, class_kernel, labels)
    with jax.named_scope("backward_sums"):
        head = lax.all_to_all(head, "tile", 0, 0, tiled=True)
    with jax.named_scope("weight_grads"):
        wide = 9 * channels
        keep, send, head = call(
            functools.partial(weights_kernel, height, numbers),
            (
                shape(in_channels, wide),
                shape(in_channels, wide, dtype=BF16),
                shape(16, channels),
            ),
            (
                pltpu.VMEM((fine_size, 3 * channels), BF16),
                pltpu.VMEM((coarse_size, 3 * channels), BF16),
                pltpu.VMEM((in_channels, wide), F32),
            ),
        )(conv, dpre, stats, head, vectors, turned, above, below)
    with jax.named_scope("over_tiles"):
        sent = lax.ppermute(send, "tile", core_pairs())
        size = in_channels // 4
        parts = call(
            first_sum_kernel, (shape(size, wide),) + (shape(size, wide, dtype=BF16),) * 3
        )(keep, sent)
        got = [lax.ppermute(parts[step], "tile", x_pairs(step)) for step in (1, 2, 3)]
        size = size // 4
        parts = call(
            next_sum_kernel, (shape(size, wide),) + (shape(size, wide, dtype=BF16),) * 3
        )(parts[0], *got)
        got = [lax.ppermute(parts[step], "tile", z_pairs(step)) for step in (1, 2, 3)]
        own = call(last_tile_kernel, shape(size, wide + channels))(parts[0], *got, head)
    with jax.named_scope("over_slides"):
        slides = lax.axis_size("slide")
        own = own + lax.ppermute(own, "slide", [(i, i ^ 1) for i in range(slides)])
        got = [
            lax.ppermute(own, "slide", [(i, (i + 2 * step) % slides) for i in range(slides)])
            for step in (1, 2, 3)
        ]
        loss, head_grads, grads = call(
            final_kernel,
            (shape(1, 1), shape(4 + classes, channels), shape(in_channels // tiles * 18, channels)),
        )(own, *got)
    conv_grads = grads.reshape(in_channels // tiles, 9, 2, channels).transpose(0, 2, 1, 3)
    return (loss.reshape(()), head_grads, conv_grads)


def solution(mesh):
    return jax.shard_map(
        per_device,
        mesh=mesh,
        in_specs=(
            P("slide", "tile", None, None),
            P("slide", "tile", None, None),
            P(),
            P(),
            P(),
            P(),
            P(),
            P(),
            P(),
            P(),
            P("slide", "tile", None),
        ),
        out_specs=(P(), P(), P("tile", None, None, None)),
        check_vma=False,
    )
```

```python
import functools

import jax
import jax.numpy as jnp
from jax import lax
from jax.experimental import pallas as pl
from jax.experimental.pallas import tpu as pltpu
from jax.sharding import PartitionSpec as P

GROUPS = 32
epsilon = 1e-05
F32 = jnp.float32
BF16 = jnp.bfloat16
VMEM_BYTES = 24 * 1024 * 1024


def call(kernel, outs, scratch=(), **more):
    return pl.pallas_call(
        kernel,
        out_shape=outs,
        scratch_shapes=list(scratch),
        compiler_params=pltpu.CompilerParams(vmem_limit_bytes=VMEM_BYTES),
        **more,
    )


def shape(*dims, dtype=F32):
    return jax.ShapeDtypeStruct(dims, dtype)


def moved(values, step):
    count = values.shape[0]
    rows = lax.broadcasted_iota(jnp.int32, values.shape, 0)
    edge = 0 if step > 0 else count - 1
    return jnp.where(rows == edge, 0.0, pltpu.roll(values, step % count, 0))


def taps_of(kernel_ref, row_step):
    return jnp.concatenate([kernel_ref[3 * row_step + b] for b in range(3)], axis=1)


def joined(products, channels):
    left = products[:, :channels]
    middle = products[:, channels : 2 * channels]
    right = products[:, 2 * channels :]
    return moved(left, 1) + middle + moved(right, -1)


def above_below(off_ref, on_ref):
    odd = lax.axis_index("tile") % 2 == 1
    off, on = off_ref[...].astype(F32), on_ref[...].astype(F32)
    return jnp.where(odd, on, off).astype(BF16), jnp.where(odd, off, on).astype(BF16)


def levels(ref, size, axis=0):
    rest = ref.shape[axis] - size
    parts = (pl.ds(0, size), pl.ds(size, rest))
    return [ref.at[part] if axis == 0 else ref.at[:, part] for part in parts]


def channel_order(channels):
    tile = lax.axis_index("tile")
    core, z, x = tile % 2, (tile // 2) % 4, tile // 8
    row = lax.broadcasted_iota(jnp.int32, (channels, channels), 0)
    col = lax.broadcasted_iota(jnp.int32, (channels, channels), 1)
    to_core = lax.rem(core + row // 128, 2)
    to_x = lax.rem(x + lax.rem(row // 32, 4), 4)
    to_z = lax.rem(z + lax.rem(row // 8, 4), 4)
    channel = (to_x * 8 + to_z * 2 + to_core) * 8 + lax.rem(row, 8)
    return (col == channel).astype(F32).astype(BF16)


def turn(order, pixels):
    return lax.dot_general(
        order, pixels, (((1,), (1,)), ((), ())), preferred_element_type=F32
    ).astype(BF16)


def interior_kernel(
    rows_fine,
    rows_coarse,
    fine_ref,
    coarse_ref,
    fk_ref,
    ck_ref,
    fgain_ref,
    foffset_ref,
    cgain_ref,
    coffset_ref,
    bias_ref,
    conv_ref,
    turn_ref,
    vectors_ref,
):
    for at, ref in enumerate((fgain_ref, foffset_ref, cgain_ref, coffset_ref)):
        vectors_ref[at : at + 1, :] = ref[...]
        vectors_ref[4 + at : 5 + at, :] = ref[...]
    for at in range(bias_ref.shape[0]):
        vectors_ref[8 + at : 9 + at, :] = jnp.full((1, vectors_ref.shape[1]), bias_ref[at], F32)
    fine_size = fine_ref.shape[0]
    fconv_ref, cconv_ref = levels(conv_ref, fine_size)
    fturn_ref, cturn_ref = levels(turn_ref, fine_size, 1)
    level_products(coarse_ref, ck_ref, cconv_ref, rows_coarse)
    level_products(fine_ref, fk_ref, fconv_ref, rows_fine)
    order = channel_order(fine_ref.shape[1])
    cturn_ref[...] = turn(order, coarse_ref[...])
    fturn_ref[...] = turn(order, fine_ref[...])


def level_products(x_ref, k_ref, out_ref, rows):
    cols = x_ref.shape[0] // rows
    channels = k_ref.shape[2]
    for row in range(rows):
        total = None
        for a in range(3):
            source = row + a - 1
            if 0 <= source < rows:
                part = jnp.dot(
                    x_ref[source * cols : (source + 1) * cols, :],
                    taps_of(k_ref, a),
                    preferred_element_type=F32,
                )
                total = part if total is None else total + part
        out_ref[row * cols : (row + 1) * cols, :] = joined(total, channels)


def edges_kernel(
    rows_fine,
    rows_coarse,
    part_ref,
    off_ref,
    on_ref,
    fk_ref,
    ck_ref,
    conv_ref,
    stats_ref,
):
    fine_size = part_ref.shape[0] * 4 // 5
    fpart_ref, cpart_ref = levels(part_ref, fine_size)
    fconv_ref, cconv_ref = levels(conv_ref, fine_size)
    above, below = above_below(off_ref, on_ref)
    start = 0
    found = []
    for part_ref, k_ref, out_ref, rows in (
        (fpart_ref, fk_ref, fconv_ref, rows_fine),
        (cpart_ref, ck_ref, cconv_ref, rows_coarse),
    ):
        cols = part_ref.shape[0] // rows
        channels = k_ref.shape[2]
        first = jnp.zeros((1, channels), F32)
        second = jnp.zeros((1, channels), F32)
        for row in range(rows):
            value = part_ref[row * cols : (row + 1) * cols, :]
            for edge, halo, a in ((0, above, 0), (rows - 1, below, 2)):
                if row == edge:
                    value = value + joined(
                        jnp.dot(
                            halo[start : start + cols, :],
                            taps_of(k_ref, a),
                            preferred_element_type=F32,
                        ),
                        channels,
                    )
            out_ref[row * cols : (row + 1) * cols, :] = value
            first = first + jnp.sum(value, axis=0, keepdims=True)
            second = second + jnp.sum(value * value, axis=0, keepdims=True)
        found += [first, second]
        start += cols
    found = jnp.concatenate(found + [jnp.zeros_like(found[0])] * 4, axis=0)
    for tile in range(stats_ref.shape[0] // 8):
        stats_ref[8 * tile : 8 * tile + 8, :] = found


def same_group(channels):
    per_group = channels // GROUPS
    row = lax.broadcasted_iota(jnp.int32, (channels, channels), 0)
    col = lax.broadcasted_iota(jnp.int32, (channels, channels), 1)
    return (row // per_group == col // per_group).astype(F32)


def over_tiles(all_ref, count):
    return jnp.sum(all_ref[...].reshape(-1, count, all_ref.shape[1]), axis=0)


def over_group(rows, members):
    return jnp.dot(rows, members, precision=lax.Precision.HIGHEST, preferred_element_type=F32)


def norm_terms(sums, level, number):
    mean = sums[2 * level : 2 * level + 1, :] / number
    variance = sums[2 * level + 1 : 2 * level + 2, :] / number - mean * mean
    return mean, lax.rsqrt(variance + epsilon)


def loss_kernel(
    rows_fine,
    numbers,
    conv_ref,
    stats_ref,
    vectors_ref,
    class_ref,
    labels_ref,
    dpre_ref,
    head_ref,
    wide_ref,
    sum_ref,
):
    fine_size = conv_ref.shape[0] * 4 // 5
    fconv_ref, cconv_ref = levels(conv_ref, fine_size)
    fdpre_ref, cdpre_ref = levels(dpre_ref, fine_size)
    channels = conv_ref.shape[1]
    cols = fconv_ref.shape[0] // rows_fine
    half = cols // 2
    classes = class_ref.shape[0]
    sums = over_group(over_tiles(stats_ref, 8), same_group(channels))
    fmean, fscale = norm_terms(sums, 0, numbers[0])
    cmean, cscale = norm_terms(sums, 1, numbers[1])
    weights = class_ref[...]
    bias = vectors_ref[8 : 8 + classes, 0:1]
    fgain, foffset = vectors_ref[0:1, :], vectors_ref[1:2, :]
    cgain, coffset = vectors_ref[2:3, :], vectors_ref[3:4, :]
    twice = jnp.concatenate([weights.astype(F32)] * 2, axis=0).astype(BF16)
    rows_sum = [jnp.zeros((1, channels), F32) for _ in range(4)]
    class_sum = jnp.zeros((classes, channels), F32)
    loss_sum = jnp.zeros((1, 2 * cols), F32)
    tissue_sum = jnp.zeros((1, 2 * cols), F32)
    class_id = lax.broadcasted_iota(jnp.int32, (classes, 2 * cols), 0)
    for pair in range(rows_fine // 2):
        cnormed = (cconv_ref[pair * half : (pair + 1) * half, :] - cmean) * cscale
        cpre = cnormed * cgain + coffset
        cact = jnp.maximum(cpre, 0.0)
        wide_ref[pl.ds(0, half, stride=2), :] = cact
        wide_ref[pl.ds(1, half, stride=2), :] = cact
        up = wide_ref[...]
        up = jnp.concatenate([up, up], axis=0)
        here = slice(2 * pair * cols, 2 * (pair + 1) * cols)
        normed = (fconv_ref[here, :] - fmean) * fscale
        pre = normed * fgain + foffset
        merged = (jnp.maximum(pre, 0.0) + up).astype(BF16)
        logits = (
            lax.dot_general(weights, merged, (((1,), (1,)), ((), ())), preferred_element_type=F32)
            + bias
        )
        top = jnp.max(logits, axis=0, keepdims=True)
        lse = top + jnp.log(jnp.sum(jnp.exp(logits - top), axis=0, keepdims=True))
        label = jnp.concatenate(
            [labels_ref[2 * pair : 2 * pair + 1, :], labels_ref[2 * pair + 1 : 2 * pair + 2, :]],
            axis=1,
        )
        tissue = (label >= 0).astype(F32)
        onehot = (label == class_id).astype(F32)
        loss_sum = loss_sum + (lse - jnp.sum(onehot * logits, axis=0, keepdims=True)) * tissue
        tissue_sum = tissue_sum + tissue
        dlogits = (jnp.exp(logits - lse) - onehot) * tissue
        high = dlogits.astype(BF16).astype(F32)
        parts = jnp.concatenate([high, dlogits - high], axis=0).astype(BF16)
        class_part = jnp.dot(parts, merged, preferred_element_type=F32)
        class_sum = class_sum + (class_part[:classes] + class_part[classes:])
        dmerged = lax.dot_general(
            parts, twice, (((0,), (0,)), ((), ())), preferred_element_type=F32
        )
        dpre = jnp.where(pre > 0, dmerged, 0.0)
        fdpre_ref[here, :] = dpre
        rows_sum[0] = rows_sum[0] + jnp.sum(dpre * normed, axis=0, keepdims=True)
        rows_sum[1] = rows_sum[1] + jnp.sum(dpre, axis=0, keepdims=True)
        both = dmerged[:cols] + dmerged[cols:]
        sum_ref[...] = both
        dact = sum_ref[pl.ds(0, half, stride=2), :] + sum_ref[pl.ds(1, half, stride=2), :]
        dpre = jnp.where(cpre > 0, dact, 0.0)
        cdpre_ref[pair * half : (pair + 1) * half, :] = dpre
        rows_sum[2] = rows_sum[2] + jnp.sum(dpre * cnormed, axis=0, keepdims=True)
        rows_sum[3] = rows_sum[3] + jnp.sum(dpre, axis=0, keepdims=True)
    lane = lax.broadcasted_iota(jnp.int32, (1, channels), 1)
    loss_all = jnp.sum(loss_sum, axis=1, keepdims=True)
    tissue_all = jnp.sum(tissue_sum, axis=1, keepdims=True)
    counts = jnp.where(lane == 0, loss_all, jnp.where(lane == 1, tissue_all, 0.0))
    blank = jnp.zeros((11 - classes, channels), F32)
    head = jnp.concatenate(rows_sum + [class_sum, counts, blank], axis=0)
    for tile in range(head_ref.shape[0] // 16):
        head_ref[16 * tile : 16 * tile + 16, :] = head


def weights_kernel(
    rows_fine,
    numbers,
    all_conv_ref,
    all_dpre_ref,
    stats_ref,
    back_ref,
    vectors_ref,
    all_turn_ref,
    off_ref,
    on_ref,
    keep_ref,
    send_ref,
    head_ref,
    fd_ref,
    cd_ref,
    wide_ref,
):
    fine_size = fd_ref.shape[0]
    fconv_ref, cconv_ref = levels(all_conv_ref, fine_size)
    fdpre_ref, cdpre_ref = levels(all_dpre_ref, fine_size)
    fturn_ref, cturn_ref = levels(all_turn_ref, fine_size, 1)
    channels = all_conv_ref.shape[1]
    members = same_group(channels)
    sums = over_group(over_tiles(stats_ref, 8), members)
    back = over_tiles(back_ref, 16)
    head_ref[...] = back
    kept = keep_ref.shape[0] // 16
    order = channel_order(off_ref.shape[1])
    above, below = [turn(order, rows) for rows in above_below(off_ref, on_ref)]
    start = 0
    for level, (conv_ref, dpre_ref, turn_ref, d_ref, rows) in enumerate(
        (
            (fconv_ref, fdpre_ref, fturn_ref, fd_ref, rows_fine),
            (cconv_ref, cdpre_ref, cturn_ref, cd_ref, rows_fine // 2),
        )
    ):
        size = conv_ref.shape[0]
        cols = size // rows
        mean, scale = norm_terms(sums, level, numbers[level])
        gain = vectors_ref[2 * level : 2 * level + 1, :]
        means = over_group(back[2 * level : 2 * level + 2, :] * gain, members) / numbers[level]
        with_normed, plain = means[0:1, :], means[1:2, :]
        for row in range(rows):
            here = slice(row * cols, (row + 1) * cols)
            normed = (conv_ref[here, :] - mean) * scale
            dconv = (dpre_ref[here, :] * gain - plain - normed * with_normed) * scale
            d_ref[here, :channels] = moved(dconv, -1).astype(BF16)
            d_ref[here, channels : 2 * channels] = dconv.astype(BF16)
            d_ref[here, 2 * channels :] = moved(dconv, 1).astype(BF16)
        for a in range(3):
            if a == 0:
                product = jnp.dot(
                    turn_ref[:, : size - cols], d_ref[cols:, :], preferred_element_type=F32
                ) + jnp.dot(
                    above[:, start : start + cols], d_ref[:cols, :], preferred_element_type=F32
                )
            elif a == 1:
                product = jnp.dot(turn_ref[...], d_ref[...], preferred_element_type=F32)
            else:
                product = jnp.dot(
                    turn_ref[:, cols:], d_ref[: size - cols, :], preferred_element_type=F32
                ) + jnp.dot(
                    below[:, start : start + cols],
                    d_ref[size - cols :, :],
                    preferred_element_type=F32,
                )
            wide = product.shape[1]
            span = slice(a * wide, (a + 1) * wide)
            for block in range(product.shape[0] // 8):
                piece = product[8 * block : 8 * block + 8, :]
                at = 16 * (block % kept) + 8 * level
                to_ref = keep_ref if block < kept else wide_ref
                to_ref[at : at + 8, span] = piece
        start += cols
    send_ref[...] = wide_ref[...].astype(BF16)


def first_sum_kernel(keep_ref, sent_ref, own_ref, *out_refs):
    size = own_ref.shape[0]
    own_ref[...] = keep_ref[:size, :] + sent_ref[:size, :].astype(F32)
    for at, out_ref in enumerate(out_refs):
        here = slice((at + 1) * size, (at + 2) * size)
        out_ref[...] = (keep_ref[here, :] + sent_ref[here, :].astype(F32)).astype(BF16)


def next_sum_kernel(keep_ref, one_ref, two_ref, three_ref, own_ref, *out_refs):
    size = own_ref.shape[0]
    for at, out_ref in enumerate((own_ref, *out_refs)):
        here = slice(at * size, (at + 1) * size)
        out_ref[...] = (
            (keep_ref[here, :] + one_ref[here, :].astype(F32))
            + (two_ref[here, :].astype(F32) + three_ref[here, :].astype(F32))
        ).astype(out_ref.dtype)


def last_tile_kernel(keep_ref, one_ref, two_ref, three_ref, head_ref, out_ref):
    wide = keep_ref.shape[1]
    out_ref[:, :wide] = (keep_ref[...] + one_ref[...].astype(F32)) + (
        two_ref[...].astype(F32) + three_ref[...].astype(F32)
    )
    out_ref[:, wide:] = head_ref[...]


def final_kernel(own_ref, one_ref, two_ref, three_ref, loss_ref, head_ref, grads_ref):
    whole = (own_ref[...] + two_ref[...]) + (one_ref[...] + three_ref[...])
    rows = head_ref.shape[0]
    channels = head_ref.shape[1]
    wide = whole.shape[1] - channels
    head = whole[:, wide:]
    total = head[rows : rows + 1, 1:2]
    loss_ref[...] = head[rows : rows + 1, 0:1] / total
    head_ref[...] = head[:rows, :] / total
    taps = wide // channels
    for level in range(2):
        for tap in range(taps):
            grads_ref[pl.ds(2 * tap + level, 8, stride=2 * taps), :] = (
                whole[8 * level : 8 * level + 8, tap * channels : (tap + 1) * channels] / total
            )


def swaps(firsts):
    return [pair for i in firsts for pair in ((i, i + 1), (i + 1, i))]


def core_pairs():
    return [(i, i ^ 1) for i in range(32)]


def x_pairs(step):
    return [(i, (i // 8 + step) % 4 * 8 + i % 8) for i in range(32)]


def z_pairs(step):
    return [(i, i // 8 * 8 + (i // 2 + step) % 4 * 2 + i % 2) for i in range(32)]


def per_device(
    fine_level,
    coarse_level,
    fine_kernel,
    coarse_kernel,
    fine_gain,
    fine_offset,
    coarse_gain,
    coarse_offset,
    class_kernel,
    class_offset,
    tissue_labels,
):
    tiles = lax.axis_size("tile")
    in_channels, _, channels = fine_kernel.shape
    _, height, width, _ = fine_level.shape
    classes = class_kernel.shape[0]
    numbers = (
        float(height * tiles * width * (channels // GROUPS)),
        float(height * tiles * width * (channels // GROUPS) // 4),
    )
    fine_size, coarse_size = height * width, height * width // 4
    pixels = fine_size + coarse_size
    fine = fine_level.reshape(fine_size, in_channels)
    coarse = coarse_level.reshape(coarse_size, in_channels)
    fk = fine_kernel.transpose(1, 0, 2)
    ck = coarse_kernel.transpose(1, 0, 2)
    labels = tissue_labels[0]
    vectors = [fine_gain, fine_offset, coarse_gain, coarse_offset]
    vectors = [vector[None, :] for vector in vectors]

    with jax.named_scope("halo"):
        odd = (lax.axis_index("tile") & 1).astype(jnp.uint32)

        def edge_rows(last):
            parts = []
            for rows, size in ((fine, width), (coarse, width // 2)):
                start = last * jnp.uint32(rows.shape[0] - size)
                parts.append(lax.dynamic_slice(rows, (start, jnp.uint32(0)), (size, in_channels)))
            return jnp.concatenate(parts)

        off, on = edge_rows(odd), edge_rows(1 - odd)
        off = lax.ppermute(off, "tile", swaps(range(1, tiles - 1, 2)))
        on = lax.ppermute(on, "tile", swaps(range(0, tiles, 2)))
    with jax.named_scope("forward"):
        whole = pl.BlockSpec(memory_space=pltpu.VMEM)
        part, turned, vectors = call(
            functools.partial(interior_kernel, height, height // 2),
            (
                shape(pixels, channels),
                shape(in_channels, pixels, dtype=BF16),
                shape(8 + classes, channels),
            ),
            in_specs=[whole] * 8 + [pl.BlockSpec(memory_space=pltpu.SMEM)],
        )(fine, coarse, fk, ck, *vectors, class_offset)
        conv, stats = call(
            functools.partial(edges_kernel, height, height // 2),
            (shape(pixels, channels), shape(8 * tiles, channels)),
            input_output_aliases={0: 0},
        )(part, off, on, fk, ck)
    with jax.named_scope("forward_sums"):
        stats = lax.all_to_all(stats, "tile", 0, 0, tiled=True)
    with jax.named_scope("loss_and_head"):
        dpre, head = call(
            functools.partial(loss_kernel, height, numbers),
            (shape(pixels, channels), shape(16 * tiles, channels)),
            (pltpu.VMEM((width, channels), F32), pltpu.VMEM((width, channels), F32)),
        )(conv, stats, vectors, class_kernel, labels)
    with jax.named_scope("backward_sums"):
        head = lax.all_to_all(head, "tile", 0, 0, tiled=True)
    with jax.named_scope("weight_grads"):
        wide = 9 * channels
        keep, send, head = call(
            functools.partial(weights_kernel, height, numbers),
            (
                shape(in_channels, wide),
                shape(in_channels, wide, dtype=BF16),
                shape(16, channels),
            ),
            (
                pltpu.VMEM((fine_size, 3 * channels), BF16),
                pltpu.VMEM((coarse_size, 3 * channels), BF16),
                pltpu.VMEM((in_channels, wide), F32),
            ),
        )(conv, dpre, stats, head, vectors, turned, off, on)
    with jax.named_scope("over_tiles"):
        sent = lax.ppermute(send, "tile", core_pairs())
        size = in_channels // 4
        parts = call(
            first_sum_kernel, (shape(size, wide),) + (shape(size, wide, dtype=BF16),) * 3
        )(keep, sent)
        got = [lax.ppermute(parts[step], "tile", x_pairs(step)) for step in (1, 2, 3)]
        size = size // 4
        parts = call(
            next_sum_kernel, (shape(size, wide),) + (shape(size, wide, dtype=BF16),) * 3
        )(parts[0], *got)
        got = [lax.ppermute(parts[step], "tile", z_pairs(step)) for step in (1, 2, 3)]
        own = call(last_tile_kernel, shape(size, wide + channels))(parts[0], *got, head)
    with jax.named_scope("over_slides"):
        slides = lax.axis_size("slide")
        own = own + lax.ppermute(own, "slide", [(i, i ^ 1) for i in range(slides)])
        got = [
            lax.ppermute(own, "slide", [(i, (i + 2 * step) % slides) for i in range(slides)])
            for step in (1, 2, 3)
        ]
        loss, head_grads, grads = call(
            final_kernel,
            (shape(1, 1), shape(4 + classes, channels), shape(in_channels // tiles * 18, channels)),
        )(own, *got)
    conv_grads = grads.reshape(in_channels // tiles, 9, 2, channels).transpose(0, 2, 1, 3)
    return (loss.reshape(()), head_grads, conv_grads)


def solution(mesh):
    return jax.shard_map(
        per_device,
        mesh=mesh,
        in_specs=(
            P("slide", "tile", None, None),
            P("slide", "tile", None, None),
            P(),
            P(),
            P(),
            P(),
            P(),
            P(),
            P(),
            P(),
            P("slide", "tile", None),
        ),
        out_specs=(P(), P(), P("tile", None, None, None)),
        check_vma=False,
    )
```

```python
import functools

import jax
import jax.numpy as jnp
from jax import lax
from jax.experimental import pallas as pl
from jax.experimental.pallas import tpu as pltpu
from jax.sharding import PartitionSpec as P

GROUPS = 32
epsilon = 1e-05
F32 = jnp.float32
BF16 = jnp.bfloat16
VMEM_BYTES = 24 * 1024 * 1024


def call(kernel, outs, scratch=(), **more):
    return pl.pallas_call(
        kernel,
        out_shape=outs,
        scratch_shapes=list(scratch),
        compiler_params=pltpu.CompilerParams(vmem_limit_bytes=VMEM_BYTES),
        **more,
    )


def shape(*dims, dtype=F32):
    return jax.ShapeDtypeStruct(dims, dtype)


def moved(values, step):
    count = values.shape[0]
    rows = lax.broadcasted_iota(jnp.int32, values.shape, 0)
    edge = 0 if step > 0 else count - 1
    return jnp.where(rows == edge, 0.0, pltpu.roll(values, step % count, 0))


def taps_of(kernel_ref, row_step):
    return jnp.concatenate([kernel_ref[3 * row_step + b] for b in range(3)], axis=1)


def joined(products, channels):
    left = products[:, :channels]
    middle = products[:, channels : 2 * channels]
    right = products[:, 2 * channels :]
    return moved(left, 1) + middle + moved(right, -1)


def above_below(off_ref, on_ref):
    odd = lax.axis_index("tile") % 2 == 1
    off, on = off_ref[...].astype(F32), on_ref[...].astype(F32)
    return jnp.where(odd, on, off).astype(BF16), jnp.where(odd, off, on).astype(BF16)


def levels(ref, size, axis=0):
    rest = ref.shape[axis] - size
    parts = (pl.ds(0, size), pl.ds(size, rest))
    return [ref.at[part] if axis == 0 else ref.at[:, part] for part in parts]


def channel_order(channels):
    tile = lax.axis_index("tile")
    core, z, x = tile % 2, (tile // 2) % 4, tile // 8
    row = lax.broadcasted_iota(jnp.int32, (channels, channels), 0)
    col = lax.broadcasted_iota(jnp.int32, (channels, channels), 1)
    to_core = lax.rem(core + row // 128, 2)
    to_x = lax.rem(x + lax.rem(row // 32, 4), 4)
    to_z = lax.rem(z + lax.rem(row // 8, 4), 4)
    channel = (to_x * 8 + to_z * 2 + to_core) * 8 + lax.rem(row, 8)
    return (col == channel).astype(F32).astype(BF16)


def turn(order, pixels):
    return lax.dot_general(
        order, pixels, (((1,), (1,)), ((), ())), preferred_element_type=F32
    ).astype(BF16)


def interior_kernel(
    rows_fine,
    rows_coarse,
    fine_ref,
    coarse_ref,
    fk_ref,
    ck_ref,
    fgain_ref,
    foffset_ref,
    cgain_ref,
    coffset_ref,
    bias_ref,
    conv_ref,
    turn_ref,
    vectors_ref,
):
    for at, ref in enumerate((fgain_ref, foffset_ref, cgain_ref, coffset_ref)):
        vectors_ref[at : at + 1, :] = ref[...]
        vectors_ref[4 + at : 5 + at, :] = ref[...]
    for at in range(bias_ref.shape[0]):
        vectors_ref[8 + at : 9 + at, :] = jnp.full((1, vectors_ref.shape[1]), bias_ref[at], F32)
    fine_size = fine_ref.shape[0]
    fconv_ref, cconv_ref = levels(conv_ref, fine_size)
    fturn_ref, cturn_ref = levels(turn_ref, fine_size, 1)
    level_products(coarse_ref, ck_ref, cconv_ref, rows_coarse)
    level_products(fine_ref, fk_ref, fconv_ref, rows_fine)
    order = channel_order(fine_ref.shape[1])
    cturn_ref[...] = turn(order, coarse_ref[...])
    fturn_ref[...] = turn(order, fine_ref[...])


def level_products(x_ref, k_ref, out_ref, rows):
    cols = x_ref.shape[0] // rows
    channels = k_ref.shape[2]
    for row in range(rows):
        total = None
        for a in range(3):
            source = row + a - 1
            if 0 <= source < rows:
                part = jnp.dot(
                    x_ref[source * cols : (source + 1) * cols, :],
                    taps_of(k_ref, a),
                    preferred_element_type=F32,
                )
                total = part if total is None else total + part
        out_ref[row * cols : (row + 1) * cols, :] = joined(total, channels)


def edges_kernel(
    rows_fine,
    rows_coarse,
    part_ref,
    off_ref,
    on_ref,
    fk_ref,
    ck_ref,
    conv_ref,
    stats_ref,
):
    fine_size = part_ref.shape[0] * 4 // 5
    fpart_ref, cpart_ref = levels(part_ref, fine_size)
    fconv_ref, cconv_ref = levels(conv_ref, fine_size)
    above, below = above_below(off_ref, on_ref)
    start = 0
    found = []
    for part_ref, k_ref, out_ref, rows in (
        (fpart_ref, fk_ref, fconv_ref, rows_fine),
        (cpart_ref, ck_ref, cconv_ref, rows_coarse),
    ):
        cols = part_ref.shape[0] // rows
        channels = k_ref.shape[2]
        first = jnp.zeros((1, channels), F32)
        second = jnp.zeros((1, channels), F32)
        for row in range(rows):
            value = part_ref[row * cols : (row + 1) * cols, :]
            for edge, halo, a in ((0, above, 0), (rows - 1, below, 2)):
                if row == edge:
                    value = value + joined(
                        jnp.dot(
                            halo[start : start + cols, :],
                            taps_of(k_ref, a),
                            preferred_element_type=F32,
                        ),
                        channels,
                    )
            out_ref[row * cols : (row + 1) * cols, :] = value
            first = first + jnp.sum(value, axis=0, keepdims=True)
            second = second + jnp.sum(value * value, axis=0, keepdims=True)
        found += [first, second]
        start += cols
    found = jnp.concatenate(found + found, axis=0)
    for pair in range(stats_ref.shape[0] // 8):
        stats_ref[8 * pair : 8 * pair + 8, :] = found


def same_group(channels):
    per_group = channels // GROUPS
    row = lax.broadcasted_iota(jnp.int32, (channels, channels), 0)
    col = lax.broadcasted_iota(jnp.int32, (channels, channels), 1)
    return (row // per_group == col // per_group).astype(F32)


def over_tiles(all_ref, count):
    return jnp.sum(all_ref[...].astype(F32).reshape(-1, count, all_ref.shape[1]), axis=0)


def stats_sums(stats_ref, members):
    pairs = over_tiles(stats_ref, 8)
    return over_group(pairs[0:4, :] + pairs[4:8, :], members)


def lane_blocks(channels):
    per_group = channels // GROUPS
    row = lax.broadcasted_iota(jnp.int32, (channels, channels), 0)
    col = lax.broadcasted_iota(jnp.int32, (channels, channels), 1)
    block_row = lax.broadcasted_iota(jnp.int32, (per_group, channels), 0)
    block_col = lax.broadcasted_iota(jnp.int32, (per_group, channels), 1)
    gather = (row // per_group == lax.rem(col, GROUPS)).astype(F32)
    back = (lax.rem(row, GROUPS) == col // per_group).astype(F32)
    return gather, back, block_col // GROUPS == block_row


def three_parts(values):
    high = values.astype(BF16).astype(F32)
    middle = (values - high).astype(BF16).astype(F32)
    return [high, middle, values - high - middle]


def over_group(rows, members):
    return jnp.dot(rows, members, precision=lax.Precision.HIGHEST, preferred_element_type=F32)


def norm_terms(sums, level, number):
    mean = sums[2 * level : 2 * level + 1, :] / number
    variance = sums[2 * level + 1 : 2 * level + 2, :] / number - mean * mean
    return mean, lax.rsqrt(variance + epsilon)


def loss_kernel(
    rows_fine,
    numbers,
    conv_ref,
    stats_ref,
    vectors_ref,
    class_ref,
    labels_ref,
    dpre_ref,
    head_ref,
    wide_ref,
    sum_ref,
):
    fine_size = conv_ref.shape[0] * 4 // 5
    fconv_ref, cconv_ref = levels(conv_ref, fine_size)
    fdpre_ref, cdpre_ref = levels(dpre_ref, fine_size)
    channels = conv_ref.shape[1]
    cols = fconv_ref.shape[0] // rows_fine
    half = cols // 2
    classes = class_ref.shape[0]
    sums = stats_sums(stats_ref, same_group(channels))
    fmean, fscale = norm_terms(sums, 0, numbers[0])
    cmean, cscale = norm_terms(sums, 1, numbers[1])
    weights = class_ref[...]
    bias = vectors_ref[8 : 8 + classes, 0:1]
    fgain, foffset = vectors_ref[0:1, :], vectors_ref[1:2, :]
    cgain, coffset = vectors_ref[2:3, :], vectors_ref[3:4, :]
    twice = jnp.concatenate([weights.astype(F32)] * 2, axis=0).astype(BF16)
    rows_sum = [jnp.zeros((1, channels), F32) for _ in range(4)]
    class_sum = jnp.zeros((classes, channels), F32)
    loss_sum = jnp.zeros((1, 2 * cols), F32)
    tissue_sum = jnp.zeros((1, 2 * cols), F32)
    class_id = lax.broadcasted_iota(jnp.int32, (classes, 2 * cols), 0)
    for pair in range(rows_fine // 2):
        cnormed = (cconv_ref[pair * half : (pair + 1) * half, :] - cmean) * cscale
        cpre = cnormed * cgain + coffset
        cact = jnp.maximum(cpre, 0.0)
        wide_ref[pl.ds(0, half, stride=2), :] = cact
        wide_ref[pl.ds(1, half, stride=2), :] = cact
        up = wide_ref[...]
        up = jnp.concatenate([up, up], axis=0)
        here = slice(2 * pair * cols, 2 * (pair + 1) * cols)
        normed = (fconv_ref[here, :] - fmean) * fscale
        pre = normed * fgain + foffset
        merged = (jnp.maximum(pre, 0.0) + up).astype(BF16)
        logits = (
            lax.dot_general(weights, merged, (((1,), (1,)), ((), ())), preferred_element_type=F32)
            + bias
        )
        top = jnp.max(logits, axis=0, keepdims=True)
        lse = top + jnp.log(jnp.sum(jnp.exp(logits - top), axis=0, keepdims=True))
        label = jnp.concatenate(
            [labels_ref[2 * pair : 2 * pair + 1, :], labels_ref[2 * pair + 1 : 2 * pair + 2, :]],
            axis=1,
        )
        tissue = (label >= 0).astype(F32)
        onehot = (label == class_id).astype(F32)
        loss_sum = loss_sum + (lse - jnp.sum(onehot * logits, axis=0, keepdims=True)) * tissue
        tissue_sum = tissue_sum + tissue
        dlogits = (jnp.exp(logits - lse) - onehot) * tissue
        high = dlogits.astype(BF16).astype(F32)
        parts = jnp.concatenate([high, dlogits - high], axis=0).astype(BF16)
        class_part = jnp.dot(parts, merged, preferred_element_type=F32)
        class_sum = class_sum + (class_part[:classes] + class_part[classes:])
        dmerged = lax.dot_general(
            parts, twice, (((0,), (0,)), ((), ())), preferred_element_type=F32
        )
        dpre = jnp.where(pre > 0, dmerged, 0.0)
        fdpre_ref[here, :] = dpre
        rows_sum[0] = rows_sum[0] + jnp.sum(dpre * normed, axis=0, keepdims=True)
        rows_sum[1] = rows_sum[1] + jnp.sum(dpre, axis=0, keepdims=True)
        both = dmerged[:cols] + dmerged[cols:]
        sum_ref[...] = both
        dact = sum_ref[pl.ds(0, half, stride=2), :] + sum_ref[pl.ds(1, half, stride=2), :]
        dpre = jnp.where(cpre > 0, dact, 0.0)
        cdpre_ref[pair * half : (pair + 1) * half, :] = dpre
        rows_sum[2] = rows_sum[2] + jnp.sum(dpre * cnormed, axis=0, keepdims=True)
        rows_sum[3] = rows_sum[3] + jnp.sum(dpre, axis=0, keepdims=True)
    gains = (fgain, fgain, cgain, cgain)
    gather, _, own_block = lane_blocks(channels)
    spread = jnp.concatenate([row * gain for row, gain in zip(rows_sum, gains)], axis=0)
    packed = jnp.where(own_block, over_group(spread, gather), 0.0)
    packed = jnp.sum(packed, axis=0, keepdims=True)
    lane = lax.broadcasted_iota(jnp.int32, (1, channels), 1)
    scalars = jnp.zeros((1, channels), F32)
    totals = [jnp.sum(row, axis=1, keepdims=True) for row in (loss_sum, tissue_sum)]
    for at, part in enumerate(three_parts(totals[0]) + three_parts(totals[1])):
        scalars = jnp.where(lane == at, part, scalars)
    head = rows_sum + [class_sum] + three_parts(packed) + [scalars]
    head = jnp.concatenate(head, axis=0).astype(BF16)
    for tile in range(head_ref.shape[0] // 16):
        head_ref[16 * tile : 16 * tile + 16, :] = head


def weights_kernel(
    rows_fine,
    numbers,
    all_conv_ref,
    all_dpre_ref,
    stats_ref,
    back_ref,
    vectors_ref,
    all_turn_ref,
    off_ref,
    on_ref,
    keep_ref,
    send_ref,
    head_ref,
    fd_ref,
    cd_ref,
    wide_ref,
):
    fine_size = fd_ref.shape[0]
    fconv_ref, cconv_ref = levels(all_conv_ref, fine_size)
    fdpre_ref, cdpre_ref = levels(all_dpre_ref, fine_size)
    fturn_ref, cturn_ref = levels(all_turn_ref, fine_size, 1)
    channels = all_conv_ref.shape[1]
    members = same_group(channels)
    sums = stats_sums(stats_ref, members)
    back = over_tiles(back_ref, 16)
    lane = lax.broadcasted_iota(jnp.int32, (1, channels), 1)
    loss_all, tissue_all = [
        back[15:16, at : at + 1] + back[15:16, at + 1 : at + 2] + back[15:16, at + 2 : at + 3]
        for at in (0, 3)
    ]
    counts = jnp.where(lane == 0, loss_all, jnp.where(lane == 1, tissue_all, 0.0))
    head_ref[...] = jnp.concatenate([back[0:12, :], counts, jnp.zeros((3, channels), F32)], axis=0)
    _, spread, own_block = lane_blocks(channels)
    packed = back[12:13, :] + back[13:14, :] + back[14:15, :]
    back = over_group(jnp.where(own_block, packed, 0.0), spread)
    kept = keep_ref.shape[0] // 16
    order = channel_order(off_ref.shape[1])
    above, below = [turn(order, rows) for rows in above_below(off_ref, on_ref)]
    start = 0
    for level, (conv_ref, dpre_ref, turn_ref, d_ref, rows) in enumerate(
        (
            (fconv_ref, fdpre_ref, fturn_ref, fd_ref, rows_fine),
            (cconv_ref, cdpre_ref, cturn_ref, cd_ref, rows_fine // 2),
        )
    ):
        size = conv_ref.shape[0]
        cols = size // rows
        mean, scale = norm_terms(sums, level, numbers[level])
        gain = vectors_ref[2 * level : 2 * level + 1, :]
        means = back[2 * level : 2 * level + 2, :] / numbers[level]
        with_normed, plain = means[0:1, :], means[1:2, :]
        for row in range(rows):
            here = slice(row * cols, (row + 1) * cols)
            normed = (conv_ref[here, :] - mean) * scale
            dconv = (dpre_ref[here, :] * gain - plain - normed * with_normed) * scale
            d_ref[here, :channels] = moved(dconv, -1).astype(BF16)
            d_ref[here, channels : 2 * channels] = dconv.astype(BF16)
            d_ref[here, 2 * channels :] = moved(dconv, 1).astype(BF16)
        for a in range(3):
            if a == 0:
                product = jnp.dot(
                    turn_ref[:, : size - cols], d_ref[cols:, :], preferred_element_type=F32
                ) + jnp.dot(
                    above[:, start : start + cols], d_ref[:cols, :], preferred_element_type=F32
                )
            elif a == 1:
                product = jnp.dot(turn_ref[...], d_ref[...], preferred_element_type=F32)
            else:
                product = jnp.dot(
                    turn_ref[:, cols:], d_ref[: size - cols, :], preferred_element_type=F32
                ) + jnp.dot(
                    below[:, start : start + cols],
                    d_ref[size - cols :, :],
                    preferred_element_type=F32,
                )
            wide = product.shape[1]
            span = slice(a * wide, (a + 1) * wide)
            for block in range(product.shape[0] // 8):
                piece = product[8 * block : 8 * block + 8, :]
                at = 16 * (block % kept) + 8 * level
                to_ref = keep_ref if block < kept else wide_ref
                to_ref[at : at + 8, span] = piece
        start += cols
    send_ref[...] = wide_ref[...].astype(BF16)


def first_sum_kernel(keep_ref, sent_ref, own_ref, *out_refs):
    size = own_ref.shape[0]
    own_ref[...] = keep_ref[:size, :] + sent_ref[:size, :].astype(F32)
    for at, out_ref in enumerate(out_refs):
        here = slice((at + 1) * size, (at + 2) * size)
        out_ref[...] = (keep_ref[here, :] + sent_ref[here, :].astype(F32)).astype(BF16)


def next_sum_kernel(keep_ref, one_ref, two_ref, three_ref, own_ref, *out_refs):
    size = own_ref.shape[0]
    for at, out_ref in enumerate((own_ref, *out_refs)):
        here = slice(at * size, (at + 1) * size)
        out_ref[...] = (
            (keep_ref[here, :] + one_ref[here, :].astype(F32))
            + (two_ref[here, :].astype(F32) + three_ref[here, :].astype(F32))
        ).astype(out_ref.dtype)


def last_tile_kernel(keep_ref, one_ref, two_ref, three_ref, head_ref, out_ref):
    wide = keep_ref.shape[1]
    out_ref[:, :wide] = (keep_ref[...] + one_ref[...].astype(F32)) + (
        two_ref[...].astype(F32) + three_ref[...].astype(F32)
    )
    out_ref[:, wide:] = head_ref[...]


def final_kernel(own_ref, one_ref, two_ref, three_ref, loss_ref, head_ref, grads_ref):
    whole = (own_ref[...] + two_ref[...]) + (one_ref[...] + three_ref[...])
    rows = head_ref.shape[0]
    channels = head_ref.shape[1]
    wide = whole.shape[1] - channels
    head = whole[:, wide:]
    total = head[rows : rows + 1, 1:2]
    loss_ref[...] = head[rows : rows + 1, 0:1] / total
    head_ref[...] = head[:rows, :] / total
    taps = wide // channels
    for level in range(2):
        for tap in range(taps):
            grads_ref[pl.ds(2 * tap + level, 8, stride=2 * taps), :] = (
                whole[8 * level : 8 * level + 8, tap * channels : (tap + 1) * channels] / total
            )


def swaps(firsts):
    return [pair for i in firsts for pair in ((i, i + 1), (i + 1, i))]


def core_pairs():
    return [(i, i ^ 1) for i in range(32)]


def x_pairs(step):
    return [(i, (i // 8 + step) % 4 * 8 + i % 8) for i in range(32)]


def z_pairs(step):
    return [(i, i // 8 * 8 + (i // 2 + step) % 4 * 2 + i % 2) for i in range(32)]


def per_device(
    fine_level,
    coarse_level,
    fine_kernel,
    coarse_kernel,
    fine_gain,
    fine_offset,
    coarse_gain,
    coarse_offset,
    class_kernel,
    class_offset,
    tissue_labels,
):
    tiles = lax.axis_size("tile")
    in_channels, _, channels = fine_kernel.shape
    _, height, width, _ = fine_level.shape
    classes = class_kernel.shape[0]
    numbers = (
        float(height * tiles * width * (channels // GROUPS)),
        float(height * tiles * width * (channels // GROUPS) // 4),
    )
    fine_size, coarse_size = height * width, height * width // 4
    pixels = fine_size + coarse_size
    fine = fine_level.reshape(fine_size, in_channels)
    coarse = coarse_level.reshape(coarse_size, in_channels)
    fk = fine_kernel.transpose(1, 0, 2)
    ck = coarse_kernel.transpose(1, 0, 2)
    labels = tissue_labels[0]
    vectors = [fine_gain, fine_offset, coarse_gain, coarse_offset]
    vectors = [vector[None, :] for vector in vectors]

    with jax.named_scope("halo"):
        odd = (lax.axis_index("tile") & 1).astype(jnp.uint32)

        def edge_rows(last):
            parts = []
            for rows, size in ((fine, width), (coarse, width // 2)):
                start = last * jnp.uint32(rows.shape[0] - size)
                parts.append(lax.dynamic_slice(rows, (start, jnp.uint32(0)), (size, in_channels)))
            return jnp.concatenate(parts)

        off, on = edge_rows(odd), edge_rows(1 - odd)
        off = lax.ppermute(off, "tile", swaps(range(1, tiles - 1, 2)))
        on = lax.ppermute(on, "tile", swaps(range(0, tiles, 2)))
    with jax.named_scope("forward"):
        whole = pl.BlockSpec(memory_space=pltpu.VMEM)
        part, turned, vectors = call(
            functools.partial(interior_kernel, height, height // 2),
            (
                shape(pixels, channels),
                shape(in_channels, pixels, dtype=BF16),
                shape(8 + classes, channels),
            ),
            in_specs=[whole] * 8 + [pl.BlockSpec(memory_space=pltpu.SMEM)],
        )(fine, coarse, fk, ck, *vectors, class_offset)
        conv, stats = call(
            functools.partial(edges_kernel, height, height // 2),
            (shape(pixels, channels), shape(4 * tiles, channels)),
            input_output_aliases={0: 0},
        )(part, off, on, fk, ck)
    with jax.named_scope("forward_sums"):
        stats = lax.all_to_all(stats, "tile", 0, 0, tiled=True)
    with jax.named_scope("loss_and_head"):
        dpre, head = call(
            functools.partial(loss_kernel, height, numbers),
            (shape(pixels, channels), shape(16 * tiles, channels, dtype=BF16)),
            (pltpu.VMEM((width, channels), F32), pltpu.VMEM((width, channels), F32)),
        )(conv, stats, vectors, class_kernel, labels)
    with jax.named_scope("backward_sums"):
        head = lax.all_to_all(head, "tile", 0, 0, tiled=True)
    with jax.named_scope("weight_grads"):
        wide = 9 * channels
        keep, send, head = call(
            functools.partial(weights_kernel, height, numbers),
            (
                shape(in_channels, wide),
                shape(in_channels, wide, dtype=BF16),
                shape(16, channels),
            ),
            (
                pltpu.VMEM((fine_size, 3 * channels), BF16),
                pltpu.VMEM((coarse_size, 3 * channels), BF16),
                pltpu.VMEM((in_channels, wide), F32),
            ),
        )(conv, dpre, stats, head, vectors, turned, off, on)
    with jax.named_scope("over_tiles"):
        sent = lax.ppermute(send, "tile", core_pairs())
        size = in_channels // 4
        parts = call(
            first_sum_kernel, (shape(size, wide),) + (shape(size, wide, dtype=BF16),) * 3
        )(keep, sent)
        got = [lax.ppermute(parts[step], "tile", x_pairs(step)) for step in (1, 2, 3)]
        size = size // 4
        parts = call(
            next_sum_kernel, (shape(size, wide),) + (shape(size, wide, dtype=BF16),) * 3
        )(parts[0], *got)
        got = [lax.ppermute(parts[step], "tile", z_pairs(step)) for step in (1, 2, 3)]
        own = call(last_tile_kernel, shape(size, wide + channels))(parts[0], *got, head)
    with jax.named_scope("over_slides"):
        slides = lax.axis_size("slide")
        own = own + lax.ppermute(own, "slide", [(i, i ^ 1) for i in range(slides)])
        got = [
            lax.ppermute(own, "slide", [(i, (i + 2 * step) % slides) for i in range(slides)])
            for step in (1, 2, 3)
        ]
        loss, head_grads, grads = call(
            final_kernel,
            (shape(1, 1), shape(4 + classes, channels), shape(in_channels // tiles * 18, channels)),
        )(own, *got)
    conv_grads = grads.reshape(in_channels // tiles, 9, 2, channels).transpose(0, 2, 1, 3)
    return (loss.reshape(()), head_grads, conv_grads)


def solution(mesh):
    return jax.shard_map(
        per_device,
        mesh=mesh,
        in_specs=(
            P("slide", "tile", None, None),
            P("slide", "tile", None, None),
            P(),
            P(),
            P(),
            P(),
            P(),
            P(),
            P(),
            P(),
            P("slide", "tile", None),
        ),
        out_specs=(P(), P(), P("tile", None, None, None)),
        check_vma=False,
    )
```

```python
import functools

import jax
import jax.numpy as jnp
from jax import lax
from jax.experimental import pallas as pl
from jax.experimental.pallas import tpu as pltpu
from jax.sharding import PartitionSpec as P

GROUPS = 32
epsilon = 1e-05
F32 = jnp.float32
BF16 = jnp.bfloat16
VMEM_BYTES = 24 * 1024 * 1024


def call(kernel, outs, scratch=(), **more):
    return pl.pallas_call(
        kernel,
        out_shape=outs,
        scratch_shapes=list(scratch),
        compiler_params=pltpu.CompilerParams(vmem_limit_bytes=VMEM_BYTES),
        **more,
    )


def shape(*dims, dtype=F32):
    return jax.ShapeDtypeStruct(dims, dtype)


def moved(values, step):
    count = values.shape[0]
    rows = lax.broadcasted_iota(jnp.int32, values.shape, 0)
    edge = 0 if step > 0 else count - 1
    return jnp.where(rows == edge, 0.0, pltpu.roll(values, step % count, 0))


def taps_of(kernel_ref, row_step):
    return jnp.concatenate([kernel_ref[3 * row_step + b] for b in range(3)], axis=1)


def joined(products, channels):
    left = products[:, :channels]
    middle = products[:, channels : 2 * channels]
    right = products[:, 2 * channels :]
    return moved(left, 1) + middle + moved(right, -1)


def above_below(off_ref, on_ref):
    odd = lax.axis_index("tile") % 2 == 1
    off, on = off_ref[...].astype(F32), on_ref[...].astype(F32)
    return jnp.where(odd, on, off).astype(BF16), jnp.where(odd, off, on).astype(BF16)


def levels(ref, size, axis=0):
    rest = ref.shape[axis] - size
    parts = (pl.ds(0, size), pl.ds(size, rest))
    return [ref.at[part] if axis == 0 else ref.at[:, part] for part in parts]


def channel_order(channels):
    tile = lax.axis_index("tile")
    core, z, x = tile % 2, (tile // 2) % 4, tile // 8
    row = lax.broadcasted_iota(jnp.int32, (channels, channels), 0)
    col = lax.broadcasted_iota(jnp.int32, (channels, channels), 1)
    to_core = lax.rem(core + row // 128, 2)
    to_x = lax.rem(x + lax.rem(row // 32, 4), 4)
    to_z = lax.rem(z + lax.rem(row // 8, 4), 4)
    channel = (to_x * 8 + to_z * 2 + to_core) * 8 + lax.rem(row, 8)
    return (col == channel).astype(F32).astype(BF16)


def turn(order, pixels):
    return lax.dot_general(
        order, pixels, (((1,), (1,)), ((), ())), preferred_element_type=F32
    ).astype(BF16)


def interior_kernel(
    rows_fine,
    rows_coarse,
    fine_ref,
    coarse_ref,
    fk_ref,
    ck_ref,
    fgain_ref,
    foffset_ref,
    cgain_ref,
    coffset_ref,
    bias_ref,
    conv_ref,
    turn_ref,
    vectors_ref,
):
    for at, ref in enumerate((fgain_ref, foffset_ref, cgain_ref, coffset_ref)):
        vectors_ref[at : at + 1, :] = ref[...]
        vectors_ref[4 + at : 5 + at, :] = ref[...]
    for at in range(bias_ref.shape[0]):
        vectors_ref[8 + at : 9 + at, :] = jnp.full((1, vectors_ref.shape[1]), bias_ref[at], F32)
    fine_size = fine_ref.shape[0]
    fconv_ref, cconv_ref = levels(conv_ref, fine_size)
    fturn_ref, cturn_ref = levels(turn_ref, fine_size, 1)
    level_products(coarse_ref, ck_ref, cconv_ref, rows_coarse)
    level_products(fine_ref, fk_ref, fconv_ref, rows_fine)
    order = channel_order(fine_ref.shape[1])
    cturn_ref[...] = turn(order, coarse_ref[...])
    fturn_ref[...] = turn(order, fine_ref[...])


def level_products(x_ref, k_ref, out_ref, rows):
    cols = x_ref.shape[0] // rows
    channels = k_ref.shape[2]
    for row in range(rows):
        total = None
        for a in range(3):
            source = row + a - 1
            if 0 <= source < rows:
                part = jnp.dot(
                    x_ref[source * cols : (source + 1) * cols, :],
                    taps_of(k_ref, a),
                    preferred_element_type=F32,
                )
                total = part if total is None else total + part
        out_ref[row * cols : (row + 1) * cols, :] = joined(total, channels)


def edges_kernel(
    rows_fine,
    rows_coarse,
    part_ref,
    off_ref,
    on_ref,
    fk_ref,
    ck_ref,
    conv_ref,
    stats_ref,
):
    fine_size = part_ref.shape[0] * 4 // 5
    fpart_ref, cpart_ref = levels(part_ref, fine_size)
    fconv_ref, cconv_ref = levels(conv_ref, fine_size)
    above, below = above_below(off_ref, on_ref)
    start = 0
    found = []
    for part_ref, k_ref, out_ref, rows in (
        (fpart_ref, fk_ref, fconv_ref, rows_fine),
        (cpart_ref, ck_ref, cconv_ref, rows_coarse),
    ):
        cols = part_ref.shape[0] // rows
        channels = k_ref.shape[2]
        first = jnp.zeros((1, channels), F32)
        second = jnp.zeros((1, channels), F32)
        for row in range(rows):
            value = part_ref[row * cols : (row + 1) * cols, :]
            for edge, halo, a in ((0, above, 0), (rows - 1, below, 2)):
                if row == edge:
                    value = value + joined(
                        jnp.dot(
                            halo[start : start + cols, :],
                            taps_of(k_ref, a),
                            preferred_element_type=F32,
                        ),
                        channels,
                    )
            out_ref[row * cols : (row + 1) * cols, :] = value
            first = first + jnp.sum(value, axis=0, keepdims=True)
            second = second + jnp.sum(value * value, axis=0, keepdims=True)
        found += [first, second]
        start += cols
    found = jnp.concatenate(found + found, axis=0)
    for pair in range(stats_ref.shape[0] // 8):
        stats_ref[8 * pair : 8 * pair + 8, :] = found


def same_group(channels):
    per_group = channels // GROUPS
    row = lax.broadcasted_iota(jnp.int32, (channels, channels), 0)
    col = lax.broadcasted_iota(jnp.int32, (channels, channels), 1)
    return (row // per_group == col // per_group).astype(F32)


def over_tiles(all_ref, count):
    return jnp.sum(all_ref[...].astype(F32).reshape(-1, count, all_ref.shape[1]), axis=0)


def stats_sums(stats_ref, members):
    pairs = over_tiles(stats_ref, 8)
    return over_group(pairs[0:4, :] + pairs[4:8, :], members)


def lane_blocks(channels):
    per_group = channels // GROUPS
    row = lax.broadcasted_iota(jnp.int32, (channels, channels), 0)
    col = lax.broadcasted_iota(jnp.int32, (channels, channels), 1)
    block_row = lax.broadcasted_iota(jnp.int32, (per_group, channels), 0)
    block_col = lax.broadcasted_iota(jnp.int32, (per_group, channels), 1)
    gather = (row // per_group == lax.rem(col, GROUPS)).astype(F32)
    back = (lax.rem(row, GROUPS) == col // per_group).astype(F32)
    return gather, back, block_col // GROUPS == block_row


def three_parts(values):
    high = values.astype(BF16).astype(F32)
    middle = (values - high).astype(BF16).astype(F32)
    return [high, middle, values - high - middle]


def over_group(rows, members):
    return jnp.dot(rows, members, precision=lax.Precision.HIGHEST, preferred_element_type=F32)


def norm_terms(sums, level, number):
    mean = sums[2 * level : 2 * level + 1, :] / number
    variance = sums[2 * level + 1 : 2 * level + 2, :] / number - mean * mean
    return mean, lax.rsqrt(variance + epsilon)


def loss_kernel(
    rows_fine,
    numbers,
    conv_ref,
    stats_ref,
    vectors_ref,
    class_ref,
    labels_ref,
    dpre_ref,
    head_ref,
    wide_ref,
    sum_ref,
):
    fine_size = conv_ref.shape[0] * 4 // 5
    fconv_ref, cconv_ref = levels(conv_ref, fine_size)
    fdpre_ref, cdpre_ref = levels(dpre_ref, fine_size)
    channels = conv_ref.shape[1]
    cols = fconv_ref.shape[0] // rows_fine
    half = cols // 2
    classes = class_ref.shape[0]
    sums = stats_sums(stats_ref, same_group(channels))
    fmean, fscale = norm_terms(sums, 0, numbers[0])
    cmean, cscale = norm_terms(sums, 1, numbers[1])
    weights = class_ref[...]
    bias = vectors_ref[8 : 8 + classes, 0:1]
    fgain, foffset = vectors_ref[0:1, :], vectors_ref[1:2, :]
    cgain, coffset = vectors_ref[2:3, :], vectors_ref[3:4, :]
    twice = jnp.concatenate([weights.astype(F32)] * 2, axis=0).astype(BF16)
    rows_sum = [jnp.zeros((1, channels), F32) for _ in range(4)]
    class_sum = jnp.zeros((classes, channels), F32)
    loss_sum = jnp.zeros((1, 2 * cols), F32)
    tissue_sum = jnp.zeros((1, 2 * cols), F32)
    class_id = lax.broadcasted_iota(jnp.int32, (classes, 2 * cols), 0)
    for pair in range(rows_fine // 2):
        cnormed = (cconv_ref[pair * half : (pair + 1) * half, :] - cmean) * cscale
        cpre = cnormed * cgain + coffset
        cact = jnp.maximum(cpre, 0.0)
        wide_ref[pl.ds(0, half, stride=2), :] = cact
        wide_ref[pl.ds(1, half, stride=2), :] = cact
        up = wide_ref[...]
        up = jnp.concatenate([up, up], axis=0)
        here = slice(2 * pair * cols, 2 * (pair + 1) * cols)
        normed = (fconv_ref[here, :] - fmean) * fscale
        pre = normed * fgain + foffset
        merged = (jnp.maximum(pre, 0.0) + up).astype(BF16)
        logits = (
            lax.dot_general(weights, merged, (((1,), (1,)), ((), ())), preferred_element_type=F32)
            + bias
        )
        top = jnp.max(logits, axis=0, keepdims=True)
        lse = top + jnp.log(jnp.sum(jnp.exp(logits - top), axis=0, keepdims=True))
        label = jnp.concatenate(
            [labels_ref[2 * pair : 2 * pair + 1, :], labels_ref[2 * pair + 1 : 2 * pair + 2, :]],
            axis=1,
        )
        tissue = (label >= 0).astype(F32)
        onehot = (label == class_id).astype(F32)
        loss_sum = loss_sum + (lse - jnp.sum(onehot * logits, axis=0, keepdims=True)) * tissue
        tissue_sum = tissue_sum + tissue
        dlogits = (jnp.exp(logits - lse) - onehot) * tissue
        high = dlogits.astype(BF16).astype(F32)
        parts = jnp.concatenate([high, dlogits - high], axis=0).astype(BF16)
        class_part = jnp.dot(parts, merged, preferred_element_type=F32)
        class_sum = class_sum + (class_part[:classes] + class_part[classes:])
        dmerged = lax.dot_general(
            parts, twice, (((0,), (0,)), ((), ())), preferred_element_type=F32
        )
        dpre = jnp.where(pre > 0, dmerged, 0.0)
        fdpre_ref[here, :] = dpre
        rows_sum[0] = rows_sum[0] + jnp.sum(dpre * normed, axis=0, keepdims=True)
        rows_sum[1] = rows_sum[1] + jnp.sum(dpre, axis=0, keepdims=True)
        both = dmerged[:cols] + dmerged[cols:]
        sum_ref[...] = both
        dact = sum_ref[pl.ds(0, half, stride=2), :] + sum_ref[pl.ds(1, half, stride=2), :]
        dpre = jnp.where(cpre > 0, dact, 0.0)
        cdpre_ref[pair * half : (pair + 1) * half, :] = dpre
        rows_sum[2] = rows_sum[2] + jnp.sum(dpre * cnormed, axis=0, keepdims=True)
        rows_sum[3] = rows_sum[3] + jnp.sum(dpre, axis=0, keepdims=True)
    gains = (fgain, fgain, cgain, cgain)
    gather, _, own_block = lane_blocks(channels)
    spread = jnp.concatenate([row * gain for row, gain in zip(rows_sum, gains)], axis=0)
    packed = jnp.where(own_block, over_group(spread, gather), 0.0)
    packed = jnp.sum(packed, axis=0, keepdims=True)
    lane = lax.broadcasted_iota(jnp.int32, (1, channels), 1)
    scalars = jnp.zeros((1, channels), F32)
    totals = [jnp.sum(row, axis=1, keepdims=True) for row in (loss_sum, tissue_sum)]
    for at, part in enumerate(three_parts(totals[0]) + three_parts(totals[1])):
        scalars = jnp.where(lane == at, part, scalars)
    head = rows_sum + [class_sum] + three_parts(packed) + [scalars]
    head = jnp.concatenate(head, axis=0).astype(BF16)
    for tile in range(head_ref.shape[0] // 16):
        head_ref[16 * tile : 16 * tile + 16, :] = head


def weights_kernel(
    rows_fine,
    numbers,
    all_conv_ref,
    all_dpre_ref,
    stats_ref,
    back_ref,
    vectors_ref,
    all_turn_ref,
    off_ref,
    on_ref,
    keep_ref,
    send_ref,
    head_ref,
    fd_ref,
    cd_ref,
    wide_ref,
):
    fine_size = fd_ref.shape[0]
    fconv_ref, cconv_ref = levels(all_conv_ref, fine_size)
    fdpre_ref, cdpre_ref = levels(all_dpre_ref, fine_size)
    fturn_ref, cturn_ref = levels(all_turn_ref, fine_size, 1)
    channels = all_conv_ref.shape[1]
    members = same_group(channels)
    sums = stats_sums(stats_ref, members)
    back = over_tiles(back_ref, 16)
    lane = lax.broadcasted_iota(jnp.int32, (1, channels), 1)
    loss_all, tissue_all = [
        back[15:16, at : at + 1] + back[15:16, at + 1 : at + 2] + back[15:16, at + 2 : at + 3]
        for at in (0, 3)
    ]
    counts = jnp.where(lane == 0, loss_all, jnp.where(lane == 1, tissue_all, 0.0))
    head_ref[...] = jnp.concatenate([back[0:12, :], counts, jnp.zeros((3, channels), F32)], axis=0)
    _, spread, own_block = lane_blocks(channels)
    packed = back[12:13, :] + back[13:14, :] + back[14:15, :]
    back = over_group(jnp.where(own_block, packed, 0.0), spread)
    kept = keep_ref.shape[0] // 16
    order = channel_order(off_ref.shape[1])
    above, below = [turn(order, rows) for rows in above_below(off_ref, on_ref)]
    start = 0
    for level, (conv_ref, dpre_ref, turn_ref, d_ref, rows) in enumerate(
        (
            (fconv_ref, fdpre_ref, fturn_ref, fd_ref, rows_fine),
            (cconv_ref, cdpre_ref, cturn_ref, cd_ref, rows_fine // 2),
        )
    ):
        size = conv_ref.shape[0]
        cols = size // rows
        mean, scale = norm_terms(sums, level, numbers[level])
        gain = vectors_ref[2 * level : 2 * level + 1, :]
        means = back[2 * level : 2 * level + 2, :] / numbers[level]
        with_normed, plain = means[0:1, :], means[1:2, :]
        for row in range(rows):
            here = slice(row * cols, (row + 1) * cols)
            normed = (conv_ref[here, :] - mean) * scale
            dconv = (dpre_ref[here, :] * gain - plain - normed * with_normed) * scale
            d_ref[here, :channels] = moved(dconv, -1).astype(BF16)
            d_ref[here, channels : 2 * channels] = dconv.astype(BF16)
            d_ref[here, 2 * channels :] = moved(dconv, 1).astype(BF16)
        for a in range(3):
            if a == 0:
                product = jnp.dot(
                    turn_ref[:, : size - cols], d_ref[cols:, :], preferred_element_type=F32
                ) + jnp.dot(
                    above[:, start : start + cols], d_ref[:cols, :], preferred_element_type=F32
                )
            elif a == 1:
                product = jnp.dot(turn_ref[...], d_ref[...], preferred_element_type=F32)
            else:
                product = jnp.dot(
                    turn_ref[:, cols:], d_ref[: size - cols, :], preferred_element_type=F32
                ) + jnp.dot(
                    below[:, start : start + cols],
                    d_ref[size - cols :, :],
                    preferred_element_type=F32,
                )
            wide = product.shape[1]
            span = slice(a * wide, (a + 1) * wide)
            for block in range(product.shape[0] // 8):
                piece = product[8 * block : 8 * block + 8, :]
                at = 16 * (block % kept) + 8 * level
                to_ref = keep_ref if block < kept else wide_ref
                to_ref[at : at + 8, span] = piece
        start += cols
    send_ref[...] = wide_ref[...].astype(BF16)


def first_sum_kernel(keep_ref, sent_ref, own_ref, *out_refs):
    size = own_ref.shape[0]
    own_ref[...] = keep_ref[:size, :] + sent_ref[:size, :].astype(F32)
    for at, out_ref in enumerate(out_refs):
        here = slice((at + 1) * size, (at + 2) * size)
        out_ref[...] = (keep_ref[here, :] + sent_ref[here, :].astype(F32)).astype(BF16)


def next_sum_kernel(keep_ref, one_ref, two_ref, three_ref, own_ref, *out_refs):
    size = own_ref.shape[0]
    for at, out_ref in enumerate((own_ref, *out_refs)):
        here = slice(at * size, (at + 1) * size)
        out_ref[...] = (
            (keep_ref[here, :] + one_ref[here, :].astype(F32))
            + (two_ref[here, :].astype(F32) + three_ref[here, :].astype(F32))
        ).astype(out_ref.dtype)


def to_message(grads, head, out_ref):
    wide, channels = grads.shape[1], head.shape[1]
    out_ref[:, :wide] = grads.astype(BF16)
    for at, part in enumerate(three_parts(head)):
        out_ref[:, wide + at * channels : wide + (at + 1) * channels] = part.astype(BF16)


def from_message(ref, wide):
    values = ref[...].astype(F32)
    channels = (values.shape[1] - wide) // 3
    high, middle, low = [
        values[:, wide + at * channels : wide + (at + 1) * channels] for at in range(3)
    ]
    return values[:, :wide], high + middle + low


def last_tile_kernel(keep_ref, one_ref, two_ref, three_ref, head_ref, out_ref):
    grads = (keep_ref[...] + one_ref[...].astype(F32)) + (
        two_ref[...].astype(F32) + three_ref[...].astype(F32)
    )
    to_message(grads, head_ref[...], out_ref)


def pair_kernel(wide, own_ref, other_ref, out_ref):
    grads, head = from_message(own_ref, wide)
    other_grads, other_head = from_message(other_ref, wide)
    to_message(grads + other_grads, head + other_head, out_ref)


def final_kernel(own_ref, one_ref, two_ref, three_ref, loss_ref, head_ref, grads_ref):
    rows, channels = head_ref.shape
    wide = own_ref.shape[1] - 3 * channels
    parts = [from_message(ref, wide) for ref in (own_ref, one_ref, two_ref, three_ref)]
    whole, head = [(own + two) + (one + three) for own, one, two, three in zip(*parts)]
    total = head[rows : rows + 1, 1:2]
    loss_ref[...] = head[rows : rows + 1, 0:1] / total
    head_ref[...] = head[:rows, :] / total
    taps = wide // channels
    for level in range(2):
        for tap in range(taps):
            grads_ref[pl.ds(2 * tap + level, 8, stride=2 * taps), :] = (
                whole[8 * level : 8 * level + 8, tap * channels : (tap + 1) * channels] / total
            )


def swaps(firsts):
    return [pair for i in firsts for pair in ((i, i + 1), (i + 1, i))]


def core_pairs():
    return [(i, i ^ 1) for i in range(32)]


def x_pairs(step):
    return [(i, (i // 8 + step) % 4 * 8 + i % 8) for i in range(32)]


def z_pairs(step):
    return [(i, i // 8 * 8 + (i // 2 + step) % 4 * 2 + i % 2) for i in range(32)]


def per_device(
    fine_level,
    coarse_level,
    fine_kernel,
    coarse_kernel,
    fine_gain,
    fine_offset,
    coarse_gain,
    coarse_offset,
    class_kernel,
    class_offset,
    tissue_labels,
):
    tiles = lax.axis_size("tile")
    in_channels, _, channels = fine_kernel.shape
    _, height, width, _ = fine_level.shape
    classes = class_kernel.shape[0]
    numbers = (
        float(height * tiles * width * (channels // GROUPS)),
        float(height * tiles * width * (channels // GROUPS) // 4),
    )
    fine_size, coarse_size = height * width, height * width // 4
    pixels = fine_size + coarse_size
    fine = fine_level.reshape(fine_size, in_channels)
    coarse = coarse_level.reshape(coarse_size, in_channels)
    fk = fine_kernel.transpose(1, 0, 2)
    ck = coarse_kernel.transpose(1, 0, 2)
    labels = tissue_labels[0]
    vectors = [fine_gain, fine_offset, coarse_gain, coarse_offset]
    vectors = [vector[None, :] for vector in vectors]

    with jax.named_scope("halo"):
        odd = (lax.axis_index("tile") & 1).astype(jnp.uint32)

        def edge_rows(last):
            parts = []
            for rows, size in ((fine, width), (coarse, width // 2)):
                start = last * jnp.uint32(rows.shape[0] - size)
                parts.append(lax.dynamic_slice(rows, (start, jnp.uint32(0)), (size, in_channels)))
            return jnp.concatenate(parts)

        off, on = edge_rows(odd), edge_rows(1 - odd)
        off = lax.ppermute(off, "tile", swaps(range(1, tiles - 1, 2)))
        on = lax.ppermute(on, "tile", swaps(range(0, tiles, 2)))
    with jax.named_scope("forward"):
        whole = pl.BlockSpec(memory_space=pltpu.VMEM)
        part, turned, vectors = call(
            functools.partial(interior_kernel, height, height // 2),
            (
                shape(pixels, channels),
                shape(in_channels, pixels, dtype=BF16),
                shape(8 + classes, channels),
            ),
            in_specs=[whole] * 8 + [pl.BlockSpec(memory_space=pltpu.SMEM)],
        )(fine, coarse, fk, ck, *vectors, class_offset)
        conv, stats = call(
            functools.partial(edges_kernel, height, height // 2),
            (shape(pixels, channels), shape(4 * tiles, channels)),
            input_output_aliases={0: 0},
        )(part, off, on, fk, ck)
    with jax.named_scope("forward_sums"):
        stats = lax.all_to_all(stats, "tile", 0, 0, tiled=True)
    with jax.named_scope("loss_and_head"):
        dpre, head = call(
            functools.partial(loss_kernel, height, numbers),
            (shape(pixels, channels), shape(16 * tiles, channels, dtype=BF16)),
            (pltpu.VMEM((width, channels), F32), pltpu.VMEM((width, channels), F32)),
        )(conv, stats, vectors, class_kernel, labels)
    with jax.named_scope("backward_sums"):
        head = lax.all_to_all(head, "tile", 0, 0, tiled=True)
    with jax.named_scope("weight_grads"):
        wide = 9 * channels
        keep, send, head = call(
            functools.partial(weights_kernel, height, numbers),
            (
                shape(in_channels, wide),
                shape(in_channels, wide, dtype=BF16),
                shape(16, channels),
            ),
            (
                pltpu.VMEM((fine_size, 3 * channels), BF16),
                pltpu.VMEM((coarse_size, 3 * channels), BF16),
                pltpu.VMEM((in_channels, wide), F32),
            ),
        )(conv, dpre, stats, head, vectors, turned, off, on)
    with jax.named_scope("over_tiles"):
        sent = lax.ppermute(send, "tile", core_pairs())
        size = in_channels // 4
        parts = call(
            first_sum_kernel, (shape(size, wide),) + (shape(size, wide, dtype=BF16),) * 3
        )(keep, sent)
        got = [lax.ppermute(parts[step], "tile", x_pairs(step)) for step in (1, 2, 3)]
        size = size // 4
        parts = call(
            next_sum_kernel, (shape(size, wide),) + (shape(size, wide, dtype=BF16),) * 3
        )(parts[0], *got)
        got = [lax.ppermute(parts[step], "tile", z_pairs(step)) for step in (1, 2, 3)]
        message = shape(size, wide + 3 * channels, dtype=BF16)
        own = call(last_tile_kernel, message)(parts[0], *got, head)
    with jax.named_scope("over_slides"):
        slides = lax.axis_size("slide")
        other = lax.ppermute(own, "slide", [(i, i ^ 1) for i in range(slides)])
        own = call(functools.partial(pair_kernel, wide), message)(own, other)
        got = [
            lax.ppermute(own, "slide", [(i, (i + 2 * step) % slides) for i in range(slides)])
            for step in (1, 2, 3)
        ]
        loss, head_grads, grads = call(
            final_kernel,
            (shape(1, 1), shape(4 + classes, channels), shape(in_channels // tiles * 18, channels)),
        )(own, *got)
    conv_grads = grads.reshape(in_channels // tiles, 9, 2, channels).transpose(0, 2, 1, 3)
    return (loss.reshape(()), head_grads, conv_grads)


def solution(mesh):
    return jax.shard_map(
        per_device,
        mesh=mesh,
        in_specs=(
            P("slide", "tile", None, None),
            P("slide", "tile", None, None),
            P(),
            P(),
            P(),
            P(),
            P(),
            P(),
            P(),
            P(),
            P("slide", "tile", None),
        ),
        out_specs=(P(), P(), P("tile", None, None, None)),
        check_vma=False,
    )
```

```python
import functools

import jax
import jax.numpy as jnp
from jax import lax
from jax.experimental import pallas as pl
from jax.experimental.pallas import tpu as pltpu
from jax.sharding import PartitionSpec as P

GROUPS = 32
epsilon = 1e-05
F32 = jnp.float32
BF16 = jnp.bfloat16
VMEM_BYTES = 24 * 1024 * 1024


def call(kernel, outs, scratch=(), **more):
    return pl.pallas_call(
        kernel,
        out_shape=outs,
        scratch_shapes=list(scratch),
        compiler_params=pltpu.CompilerParams(vmem_limit_bytes=VMEM_BYTES),
        **more,
    )


def shape(*dims, dtype=F32):
    return jax.ShapeDtypeStruct(dims, dtype)


def moved(values, step):
    count = values.shape[0]
    rows = lax.broadcasted_iota(jnp.int32, values.shape, 0)
    edge = 0 if step > 0 else count - 1
    return jnp.where(rows == edge, 0.0, pltpu.roll(values, step % count, 0))


def taps_of(kernel_ref, row_step):
    return jnp.concatenate([kernel_ref[3 * row_step + b] for b in range(3)], axis=1)


def joined(products, channels):
    left = products[:, :channels]
    middle = products[:, channels : 2 * channels]
    right = products[:, 2 * channels :]
    return moved(left, 1) + middle + moved(right, -1)


def above_below(off_ref, on_ref):
    odd = lax.axis_index("tile") % 2 == 1
    off, on = off_ref[...].astype(F32), on_ref[...].astype(F32)
    return jnp.where(odd, on, off).astype(BF16), jnp.where(odd, off, on).astype(BF16)


def levels(ref, size, axis=0):
    rest = ref.shape[axis] - size
    parts = (pl.ds(0, size), pl.ds(size, rest))
    return [ref.at[part] if axis == 0 else ref.at[:, part] for part in parts]


def channel_order(channels):
    tile = lax.axis_index("tile")
    core, z, x = tile % 2, (tile // 2) % 4, tile // 8
    row = lax.broadcasted_iota(jnp.int32, (channels, channels), 0)
    col = lax.broadcasted_iota(jnp.int32, (channels, channels), 1)
    to_core = lax.rem(core + row // 128, 2)
    to_x = lax.rem(x + lax.rem(row // 32, 4), 4)
    to_z = lax.rem(z + lax.rem(row // 8, 4), 4)
    channel = (to_x * 8 + to_z * 2 + to_core) * 8 + lax.rem(row, 8)
    return (col == channel).astype(F32).astype(BF16)


def turn(order, pixels):
    return lax.dot_general(
        order, pixels, (((1,), (1,)), ((), ())), preferred_element_type=F32
    ).astype(BF16)


def interior_kernel(
    rows_fine,
    rows_coarse,
    fine_ref,
    coarse_ref,
    fk_ref,
    ck_ref,
    fgain_ref,
    foffset_ref,
    cgain_ref,
    coffset_ref,
    bias_ref,
    conv_ref,
    turn_ref,
    vectors_ref,
    inner_ref,
):
    for at, ref in enumerate((fgain_ref, foffset_ref, cgain_ref, coffset_ref)):
        vectors_ref[at : at + 1, :] = ref[...]
        vectors_ref[4 + at : 5 + at, :] = ref[...]
    for at in range(bias_ref.shape[0]):
        vectors_ref[8 + at : 9 + at, :] = jnp.full((1, vectors_ref.shape[1]), bias_ref[at], F32)
    fine_size = fine_ref.shape[0]
    fconv_ref, cconv_ref = levels(conv_ref, fine_size)
    fturn_ref, cturn_ref = levels(turn_ref, fine_size, 1)
    coarse_sums = level_products(coarse_ref, ck_ref, cconv_ref, rows_coarse)
    fine_sums = level_products(fine_ref, fk_ref, fconv_ref, rows_fine)
    inner_ref[...] = jnp.concatenate((fine_sums + coarse_sums) * 2, axis=0)
    order = channel_order(fine_ref.shape[1])
    cturn_ref[...] = turn(order, coarse_ref[...])
    fturn_ref[...] = turn(order, fine_ref[...])


def level_products(x_ref, k_ref, out_ref, rows):
    cols = x_ref.shape[0] // rows
    channels = k_ref.shape[2]
    sums = [jnp.zeros((1, channels), F32)] * 2
    for row in range(rows):
        total = None
        for a in range(3):
            source = row + a - 1
            if 0 <= source < rows:
                part = jnp.dot(
                    x_ref[source * cols : (source + 1) * cols, :],
                    taps_of(k_ref, a),
                    preferred_element_type=F32,
                )
                total = part if total is None else total + part
        value = joined(total, channels)
        out_ref[row * cols : (row + 1) * cols, :] = value
        if 0 < row < rows - 1:
            sums = with_sums(sums, value)
    return sums


def with_sums(sums, value):
    added = [jnp.sum(v, axis=0, keepdims=True) for v in (value, value * value)]
    return [total + part for total, part in zip(sums, added)]


def edges_kernel(
    rows_fine,
    rows_coarse,
    part_ref,
    inner_ref,
    off_ref,
    on_ref,
    fk_ref,
    ck_ref,
    edges_ref,
    stats_ref,
):
    fine_size = part_ref.shape[0] * 4 // 5
    above, below = above_below(off_ref, on_ref)
    start = 0
    found = []
    for level, (level_ref, k_ref, rows) in enumerate(
        zip(levels(part_ref, fine_size), (fk_ref, ck_ref), (rows_fine, rows_coarse))
    ):
        cols = level_ref.shape[0] // rows
        channels = k_ref.shape[2]
        sums = [inner_ref[2 * level + at : 2 * level + at + 1, :] for at in range(2)]
        for edge, (row, halo, a) in enumerate(((0, above, 0), (rows - 1, below, 2))):
            product = jnp.dot(
                halo[start : start + cols, :], taps_of(k_ref, a), preferred_element_type=F32
            )
            value = level_ref[row * cols : (row + 1) * cols, :] + joined(product, channels)
            to = 2 * start + edge * cols
            edges_ref[to : to + cols, :] = value
            sums = with_sums(sums, value)
        found += sums
        start += cols
    gather, _, own_block = lane_blocks(channels)
    stats_ref[...] = jnp.broadcast_to(packed_sums(found, gather, own_block), stats_ref.shape)


def conv_rows(part_ref, edges_ref, level, row, rows):
    wide = edges_ref.shape[0] // 3
    cols = wide // (level + 1)
    if 0 < row < rows - 1:
        return part_ref[row * cols : (row + 1) * cols, :]
    at = 2 * level * wide + (cols if row else 0)
    return edges_ref[at : at + cols, :]


def over_tiles(all_ref, count):
    return jnp.sum(all_ref[...].astype(F32).reshape(-1, count, all_ref.shape[1]), axis=0)


def stats_sums(stats_ref, channels):
    _, spread, own_block = lane_blocks(channels)
    total = jnp.sum(stats_ref[...], axis=0, keepdims=True)
    return over_group(jnp.where(own_block, total, 0.0), spread)


def packed_sums(rows, gather, own_block):
    groups = over_group(jnp.concatenate(rows, axis=0), gather)
    return jnp.sum(jnp.where(own_block, groups, 0.0), axis=0, keepdims=True)


def lane_blocks(channels):
    per_group = channels // GROUPS
    row = lax.broadcasted_iota(jnp.int32, (channels, channels), 0)
    col = lax.broadcasted_iota(jnp.int32, (channels, channels), 1)
    block_row = lax.broadcasted_iota(jnp.int32, (per_group, channels), 0)
    block_col = lax.broadcasted_iota(jnp.int32, (per_group, channels), 1)
    gather = (row // per_group == lax.rem(col, GROUPS)).astype(F32)
    back = (lax.rem(row, GROUPS) == col // per_group).astype(F32)
    return gather, back, block_col // GROUPS == block_row


def three_parts(values):
    high = values.astype(BF16).astype(F32)
    middle = (values - high).astype(BF16).astype(F32)
    return [high, middle, values - high - middle]


def over_group(rows, members):
    return jnp.dot(rows, members, precision=lax.Precision.HIGHEST, preferred_element_type=F32)


def norm_terms(sums, level, number):
    mean = sums[2 * level : 2 * level + 1, :] / number
    variance = sums[2 * level + 1 : 2 * level + 2, :] / number - mean * mean
    return mean, lax.rsqrt(variance + epsilon)


def loss_kernel(
    rows_fine,
    numbers,
    conv_ref,
    edges_ref,
    stats_ref,
    vectors_ref,
    class_ref,
    labels_ref,
    dpre_ref,
    head_ref,
    wide_ref,
    sum_ref,
):
    fine_size = conv_ref.shape[0] * 4 // 5
    fconv_ref, cconv_ref = levels(conv_ref, fine_size)
    fdpre_ref, cdpre_ref = levels(dpre_ref, fine_size)
    channels = conv_ref.shape[1]
    cols = fconv_ref.shape[0] // rows_fine
    half = cols // 2
    classes = class_ref.shape[0]
    sums = stats_sums(stats_ref, channels)
    fmean, fscale = norm_terms(sums, 0, numbers[0])
    cmean, cscale = norm_terms(sums, 1, numbers[1])
    weights = class_ref[...]
    bias = vectors_ref[8 : 8 + classes, 0:1]
    fgain, foffset = vectors_ref[0:1, :], vectors_ref[1:2, :]
    cgain, coffset = vectors_ref[2:3, :], vectors_ref[3:4, :]
    twice = jnp.concatenate([weights.astype(F32)] * 2, axis=0).astype(BF16)
    rows_sum = [jnp.zeros((1, channels), F32) for _ in range(4)]
    class_sum = jnp.zeros((classes, channels), F32)
    loss_sum = jnp.zeros((1, 2 * cols), F32)
    tissue_sum = jnp.zeros((1, 2 * cols), F32)
    class_id = lax.broadcasted_iota(jnp.int32, (classes, 2 * cols), 0)
    for pair in range(rows_fine // 2):
        cconv = conv_rows(cconv_ref, edges_ref, 1, pair, rows_fine // 2)
        cnormed = (cconv - cmean) * cscale
        cpre = cnormed * cgain + coffset
        cact = jnp.maximum(cpre, 0.0)
        wide_ref[pl.ds(0, half, stride=2), :] = cact
        wide_ref[pl.ds(1, half, stride=2), :] = cact
        up = wide_ref[...]
        up = jnp.concatenate([up, up], axis=0)
        here = slice(2 * pair * cols, 2 * (pair + 1) * cols)
        fconv = [conv_rows(fconv_ref, edges_ref, 0, 2 * pair + at, rows_fine) for at in range(2)]
        normed = (jnp.concatenate(fconv, axis=0) - fmean) * fscale
        pre = normed * fgain + foffset
        merged = (jnp.maximum(pre, 0.0) + up).astype(BF16)
        logits = (
            lax.dot_general(weights, merged, (((1,), (1,)), ((), ())), preferred_element_type=F32)
            + bias
        )
        top = jnp.max(logits, axis=0, keepdims=True)
        lse = top + jnp.log(jnp.sum(jnp.exp(logits - top), axis=0, keepdims=True))
        label = jnp.concatenate(
            [labels_ref[2 * pair : 2 * pair + 1, :], labels_ref[2 * pair + 1 : 2 * pair + 2, :]],
            axis=1,
        )
        tissue = (label >= 0).astype(F32)
        onehot = (label == class_id).astype(F32)
        loss_sum = loss_sum + (lse - jnp.sum(onehot * logits, axis=0, keepdims=True)) * tissue
        tissue_sum = tissue_sum + tissue
        dlogits = (jnp.exp(logits - lse) - onehot) * tissue
        high = dlogits.astype(BF16).astype(F32)
        parts = jnp.concatenate([high, dlogits - high], axis=0).astype(BF16)
        class_part = jnp.dot(parts, merged, preferred_element_type=F32)
        class_sum = class_sum + (class_part[:classes] + class_part[classes:])
        dmerged = lax.dot_general(
            parts, twice, (((0,), (0,)), ((), ())), preferred_element_type=F32
        )
        dpre = jnp.where(pre > 0, dmerged, 0.0)
        fdpre_ref[here, :] = dpre
        rows_sum[0] = rows_sum[0] + jnp.sum(dpre * normed, axis=0, keepdims=True)
        rows_sum[1] = rows_sum[1] + jnp.sum(dpre, axis=0, keepdims=True)
        both = dmerged[:cols] + dmerged[cols:]
        sum_ref[...] = both
        dact = sum_ref[pl.ds(0, half, stride=2), :] + sum_ref[pl.ds(1, half, stride=2), :]
        dpre = jnp.where(cpre > 0, dact, 0.0)
        cdpre_ref[pair * half : (pair + 1) * half, :] = dpre
        rows_sum[2] = rows_sum[2] + jnp.sum(dpre * cnormed, axis=0, keepdims=True)
        rows_sum[3] = rows_sum[3] + jnp.sum(dpre, axis=0, keepdims=True)
    gains = (fgain, fgain, cgain, cgain)
    gather, _, own_block = lane_blocks(channels)
    packed = packed_sums([row * gain for row, gain in zip(rows_sum, gains)], gather, own_block)
    lane = lax.broadcasted_iota(jnp.int32, (1, channels), 1)
    scalars = jnp.zeros((1, channels), F32)
    totals = [jnp.sum(row, axis=1, keepdims=True) for row in (loss_sum, tissue_sum)]
    for at, part in enumerate(three_parts(totals[0]) + three_parts(totals[1])):
        scalars = jnp.where(lane == at, part, scalars)
    head = rows_sum + [class_sum] + three_parts(packed) + [scalars]
    head = jnp.concatenate(head, axis=0).astype(BF16)
    for tile in range(head_ref.shape[0] // 16):
        head_ref[16 * tile : 16 * tile + 16, :] = head


def weights_kernel(
    rows_fine,
    numbers,
    all_conv_ref,
    edges_ref,
    all_dpre_ref,
    stats_ref,
    back_ref,
    vectors_ref,
    all_turn_ref,
    off_ref,
    on_ref,
    keep_ref,
    send_ref,
    head_ref,
    fd_ref,
    cd_ref,
    wide_ref,
):
    fine_size = fd_ref.shape[0]
    fconv_ref, cconv_ref = levels(all_conv_ref, fine_size)
    fdpre_ref, cdpre_ref = levels(all_dpre_ref, fine_size)
    fturn_ref, cturn_ref = levels(all_turn_ref, fine_size, 1)
    channels = all_conv_ref.shape[1]
    sums = stats_sums(stats_ref, channels)
    back = over_tiles(back_ref, 16)
    lane = lax.broadcasted_iota(jnp.int32, (1, channels), 1)
    loss_all, tissue_all = [
        back[15:16, at : at + 1] + back[15:16, at + 1 : at + 2] + back[15:16, at + 2 : at + 3]
        for at in (0, 3)
    ]
    counts = jnp.where(lane == 0, loss_all, jnp.where(lane == 1, tissue_all, 0.0))
    head_ref[...] = jnp.concatenate([back[0:12, :], counts, jnp.zeros((3, channels), F32)], axis=0)
    _, spread, own_block = lane_blocks(channels)
    packed = back[12:13, :] + back[13:14, :] + back[14:15, :]
    back = over_group(jnp.where(own_block, packed, 0.0), spread)
    kept = keep_ref.shape[0] // 16
    order = channel_order(off_ref.shape[1])
    above, below = [turn(order, rows) for rows in above_below(off_ref, on_ref)]
    start = 0
    for level, (conv_ref, dpre_ref, turn_ref, d_ref, rows) in enumerate(
        (
            (fconv_ref, fdpre_ref, fturn_ref, fd_ref, rows_fine),
            (cconv_ref, cdpre_ref, cturn_ref, cd_ref, rows_fine // 2),
        )
    ):
        size = conv_ref.shape[0]
        cols = size // rows
        mean, scale = norm_terms(sums, level, numbers[level])
        gain = vectors_ref[2 * level : 2 * level + 1, :]
        means = back[2 * level : 2 * level + 2, :] / numbers[level]
        with_normed, plain = means[0:1, :], means[1:2, :]
        for row in range(rows):
            here = slice(row * cols, (row + 1) * cols)
            normed = (conv_rows(conv_ref, edges_ref, level, row, rows) - mean) * scale
            dconv = (dpre_ref[here, :] * gain - plain - normed * with_normed) * scale
            d_ref[here, :channels] = moved(dconv, -1).astype(BF16)
            d_ref[here, channels : 2 * channels] = dconv.astype(BF16)
            d_ref[here, 2 * channels :] = moved(dconv, 1).astype(BF16)
        for a in range(3):
            if a == 0:
                product = jnp.dot(
                    turn_ref[:, : size - cols], d_ref[cols:, :], preferred_element_type=F32
                ) + jnp.dot(
                    above[:, start : start + cols], d_ref[:cols, :], preferred_element_type=F32
                )
            elif a == 1:
                product = jnp.dot(turn_ref[...], d_ref[...], preferred_element_type=F32)
            else:
                product = jnp.dot(
                    turn_ref[:, cols:], d_ref[: size - cols, :], preferred_element_type=F32
                ) + jnp.dot(
                    below[:, start : start + cols],
                    d_ref[size - cols :, :],
                    preferred_element_type=F32,
                )
            wide = product.shape[1]
            span = slice(a * wide, (a + 1) * wide)
            for block in range(product.shape[0] // 8):
                piece = product[8 * block : 8 * block + 8, :]
                at = 16 * (block % kept) + 8 * level
                to_ref = keep_ref if block < kept else wide_ref
                to_ref[at : at + 8, span] = piece
        start += cols
    send_ref[...] = wide_ref[...].astype(BF16)


def first_sum_kernel(keep_ref, sent_ref, own_ref, *out_refs):
    size = own_ref.shape[0]
    own_ref[...] = keep_ref[:size, :] + sent_ref[:size, :].astype(F32)
    for at, out_ref in enumerate(out_refs):
        here = slice((at + 1) * size, (at + 2) * size)
        out_ref[...] = (keep_ref[here, :] + sent_ref[here, :].astype(F32)).astype(BF16)


def next_sum_kernel(keep_ref, one_ref, two_ref, three_ref, own_ref, *out_refs):
    size = own_ref.shape[0]
    for at, out_ref in enumerate((own_ref, *out_refs)):
        here = slice(at * size, (at + 1) * size)
        out_ref[...] = (
            (keep_ref[here, :] + one_ref[here, :].astype(F32))
            + (two_ref[here, :].astype(F32) + three_ref[here, :].astype(F32))
        ).astype(out_ref.dtype)


def to_message(grads, head, out_ref):
    wide, channels = grads.shape[1], head.shape[1]
    out_ref[:, :wide] = grads.astype(BF16)
    for at, part in enumerate(three_parts(head)):
        out_ref[:, wide + at * channels : wide + (at + 1) * channels] = part.astype(BF16)


def from_message(ref, wide):
    values = ref[...].astype(F32)
    channels = (values.shape[1] - wide) // 3
    high, middle, low = [
        values[:, wide + at * channels : wide + (at + 1) * channels] for at in range(3)
    ]
    return values[:, :wide], high + middle + low


def last_tile_kernel(keep_ref, one_ref, two_ref, three_ref, head_ref, out_ref):
    grads = (keep_ref[...] + one_ref[...].astype(F32)) + (
        two_ref[...].astype(F32) + three_ref[...].astype(F32)
    )
    to_message(grads, head_ref[...], out_ref)


def pair_kernel(wide, own_ref, other_ref, out_ref):
    grads, head = from_message(own_ref, wide)
    other_grads, other_head = from_message(other_ref, wide)
    to_message(grads + other_grads, head + other_head, out_ref)


def final_kernel(own_ref, one_ref, two_ref, three_ref, loss_ref, head_ref, grads_ref):
    rows, channels = head_ref.shape
    wide = own_ref.shape[1] - 3 * channels
    parts = [from_message(ref, wide) for ref in (own_ref, one_ref, two_ref, three_ref)]
    whole, head = [(own + two) + (one + three) for own, one, two, three in zip(*parts)]
    total = head[rows : rows + 1, 1:2]
    loss_ref[...] = head[rows : rows + 1, 0:1] / total
    head_ref[...] = head[:rows, :] / total
    taps = wide // channels
    for level in range(2):
        for tap in range(taps):
            grads_ref[pl.ds(2 * tap + level, 8, stride=2 * taps), :] = (
                whole[8 * level : 8 * level + 8, tap * channels : (tap + 1) * channels] / total
            )


def swaps(firsts):
    return [pair for i in firsts for pair in ((i, i + 1), (i + 1, i))]


def core_pairs():
    return [(i, i ^ 1) for i in range(32)]


def x_pairs(step):
    return [(i, (i // 8 + step) % 4 * 8 + i % 8) for i in range(32)]


def z_pairs(step):
    return [(i, i // 8 * 8 + (i // 2 + step) % 4 * 2 + i % 2) for i in range(32)]


def per_device(
    fine_level,
    coarse_level,
    fine_kernel,
    coarse_kernel,
    fine_gain,
    fine_offset,
    coarse_gain,
    coarse_offset,
    class_kernel,
    class_offset,
    tissue_labels,
):
    tiles = lax.axis_size("tile")
    in_channels, _, channels = fine_kernel.shape
    _, height, width, _ = fine_level.shape
    classes = class_kernel.shape[0]
    numbers = (
        float(height * tiles * width * (channels // GROUPS)),
        float(height * tiles * width * (channels // GROUPS) // 4),
    )
    fine_size, coarse_size = height * width, height * width // 4
    pixels = fine_size + coarse_size
    fine = fine_level.reshape(fine_size, in_channels)
    coarse = coarse_level.reshape(coarse_size, in_channels)
    fk = fine_kernel.transpose(1, 0, 2)
    ck = coarse_kernel.transpose(1, 0, 2)
    labels = tissue_labels[0]
    vectors = [fine_gain, fine_offset, coarse_gain, coarse_offset]
    vectors = [vector[None, :] for vector in vectors]

    with jax.named_scope("halo"):
        odd = (lax.axis_index("tile") & 1).astype(jnp.uint32)

        def edge_rows(last):
            parts = []
            for rows, size in ((fine, width), (coarse, width // 2)):
                start = last * jnp.uint32(rows.shape[0] - size)
                parts.append(lax.dynamic_slice(rows, (start, jnp.uint32(0)), (size, in_channels)))
            return jnp.concatenate(parts)

        off, on = edge_rows(odd), edge_rows(1 - odd)
        off = lax.ppermute(off, "tile", swaps(range(1, tiles - 1, 2)))
        on = lax.ppermute(on, "tile", swaps(range(0, tiles, 2)))
    with jax.named_scope("forward"):
        whole = pl.BlockSpec(memory_space=pltpu.VMEM)
        conv, turned, vectors, inner = call(
            functools.partial(interior_kernel, height, height // 2),
            (
                shape(pixels, channels),
                shape(in_channels, pixels, dtype=BF16),
                shape(8 + classes, channels),
                shape(8, channels),
            ),
            in_specs=[whole] * 8 + [pl.BlockSpec(memory_space=pltpu.SMEM)],
        )(fine, coarse, fk, ck, *vectors, class_offset)
        edges, stats = call(
            functools.partial(edges_kernel, height, height // 2),
            (shape(3 * width, channels), shape(tiles, channels)),
        )(conv, inner, off, on, fk, ck)
    with jax.named_scope("forward_sums"):
        stats = lax.all_to_all(stats, "tile", 0, 0, tiled=True)
    with jax.named_scope("loss_and_head"):
        dpre, head = call(
            functools.partial(loss_kernel, height, numbers),
            (shape(pixels, channels), shape(16 * tiles, channels, dtype=BF16)),
            (pltpu.VMEM((width, channels), F32), pltpu.VMEM((width, channels), F32)),
        )(conv, edges, stats, vectors, class_kernel, labels)
    with jax.named_scope("backward_sums"):
        head = lax.all_to_all(head, "tile", 0, 0, tiled=True)
    with jax.named_scope("weight_grads"):
        wide = 9 * channels
        keep, send, head = call(
            functools.partial(weights_kernel, height, numbers),
            (
                shape(in_channels, wide),
                shape(in_channels, wide, dtype=BF16),
                shape(16, channels),
            ),
            (
                pltpu.VMEM((fine_size, 3 * channels), BF16),
                pltpu.VMEM((coarse_size, 3 * channels), BF16),
                pltpu.VMEM((in_channels, wide), F32),
            ),
        )(conv, edges, dpre, stats, head, vectors, turned, off, on)
    with jax.named_scope("over_tiles"):
        sent = lax.ppermute(send, "tile", core_pairs())
        size = in_channels // 4
        parts = call(
            first_sum_kernel, (shape(size, wide),) + (shape(size, wide, dtype=BF16),) * 3
        )(keep, sent)
        got = [lax.ppermute(parts[step], "tile", x_pairs(step)) for step in (1, 2, 3)]
        size = size // 4
        parts = call(
            next_sum_kernel, (shape(size, wide),) + (shape(size, wide, dtype=BF16),) * 3
        )(parts[0], *got)
        got = [lax.ppermute(parts[step], "tile", z_pairs(step)) for step in (1, 2, 3)]
        message = shape(size, wide + 3 * channels, dtype=BF16)
        own = call(last_tile_kernel, message)(parts[0], *got, head)
    with jax.named_scope("over_slides"):
        slides = lax.axis_size("slide")
        other = lax.ppermute(own, "slide", [(i, i ^ 1) for i in range(slides)])
        own = call(functools.partial(pair_kernel, wide), message)(own, other)
        got = [
            lax.ppermute(own, "slide", [(i, (i + 2 * step) % slides) for i in range(slides)])
            for step in (1, 2, 3)
        ]
        loss, head_grads, grads = call(
            final_kernel,
            (shape(1, 1), shape(4 + classes, channels), shape(in_channels // tiles * 18, channels)),
        )(own, *got)
    conv_grads = grads.reshape(in_channels // tiles, 9, 2, channels).transpose(0, 2, 1, 3)
    return (loss.reshape(()), head_grads, conv_grads)


def solution(mesh):
    return jax.shard_map(
        per_device,
        mesh=mesh,
        in_specs=(
            P("slide", "tile", None, None),
            P("slide", "tile", None, None),
            P(),
            P(),
            P(),
            P(),
            P(),
            P(),
            P(),
            P(),
            P("slide", "tile", None),
        ),
        out_specs=(P(), P(), P("tile", None, None, None)),
        check_vma=False,
    )
```

```python
import functools

import jax
import jax.numpy as jnp
from jax import lax
from jax.experimental import pallas as pl
from jax.experimental.pallas import tpu as pltpu
from jax.sharding import PartitionSpec as P

GROUPS = 32
epsilon = 1e-05
F32 = jnp.float32
BF16 = jnp.bfloat16
VMEM_BYTES = 24 * 1024 * 1024


def call(kernel, outs, scratch=(), **more):
    return pl.pallas_call(
        kernel,
        out_shape=outs,
        scratch_shapes=list(scratch),
        compiler_params=pltpu.CompilerParams(vmem_limit_bytes=VMEM_BYTES),
        **more,
    )


def shape(*dims, dtype=F32):
    return jax.ShapeDtypeStruct(dims, dtype)


def moved(values, step):
    count = values.shape[0]
    rows = lax.broadcasted_iota(jnp.int32, values.shape, 0)
    edge = 0 if step > 0 else count - 1
    return jnp.where(rows == edge, 0.0, pltpu.roll(values, step % count, 0))


def taps_of(kernel_ref, row_step):
    return jnp.concatenate([kernel_ref[3 * row_step + b] for b in range(3)], axis=1)


def joined(products, channels):
    left = products[:, :channels]
    middle = products[:, channels : 2 * channels]
    right = products[:, 2 * channels :]
    return moved(left, 1) + middle + moved(right, -1)


def above_below(off_ref, on_ref):
    odd = lax.axis_index("tile") % 2 == 1
    off, on = off_ref[...].astype(F32), on_ref[...].astype(F32)
    return jnp.where(odd, on, off).astype(BF16), jnp.where(odd, off, on).astype(BF16)


def levels(ref, size, axis=0):
    rest = ref.shape[axis] - size
    parts = (pl.ds(0, size), pl.ds(size, rest))
    return [ref.at[part] if axis == 0 else ref.at[:, part] for part in parts]


def channel_order(channels):
    tile = lax.axis_index("tile")
    core, z, x = tile % 2, (tile // 2) % 4, tile // 8
    row = lax.broadcasted_iota(jnp.int32, (channels, channels), 0)
    col = lax.broadcasted_iota(jnp.int32, (channels, channels), 1)
    to_core = lax.rem(core + row // 128, 2)
    to_x = lax.rem(x + lax.rem(row // 32, 4), 4)
    to_z = lax.rem(z + lax.rem(row // 8, 4), 4)
    channel = (to_x * 8 + to_z * 2 + to_core) * 8 + lax.rem(row, 8)
    return (col == channel).astype(F32).astype(BF16)


def turn(order, pixels):
    return lax.dot_general(
        order, pixels, (((1,), (1,)), ((), ())), preferred_element_type=F32
    ).astype(BF16)


def interior_kernel(
    rows_fine,
    rows_coarse,
    fine_ref,
    coarse_ref,
    fk_ref,
    ck_ref,
    fgain_ref,
    foffset_ref,
    cgain_ref,
    coffset_ref,
    bias_ref,
    conv_ref,
    turn_ref,
    vectors_ref,
    inner_ref,
):
    for at, ref in enumerate((fgain_ref, foffset_ref, cgain_ref, coffset_ref)):
        vectors_ref[at : at + 1, :] = ref[...]
        vectors_ref[4 + at : 5 + at, :] = ref[...]
    for at in range(bias_ref.shape[0]):
        vectors_ref[8 + at : 9 + at, :] = jnp.full((1, vectors_ref.shape[1]), bias_ref[at], F32)
    fine_size = fine_ref.shape[0]
    fconv_ref, cconv_ref = levels(conv_ref, fine_size)
    fturn_ref, cturn_ref = levels(turn_ref, fine_size, 1)
    coarse_sums = level_products(coarse_ref, ck_ref, cconv_ref, rows_coarse)
    fine_sums = level_products(fine_ref, fk_ref, fconv_ref, rows_fine)
    inner_ref[...] = jnp.concatenate((fine_sums + coarse_sums) * 2, axis=0)
    order = channel_order(fine_ref.shape[1])
    cturn_ref[...] = turn(order, coarse_ref[...])
    fturn_ref[...] = turn(order, fine_ref[...])


def level_products(x_ref, k_ref, out_ref, rows):
    cols = x_ref.shape[0] // rows
    channels = k_ref.shape[2]
    sums = [jnp.zeros((1, channels), F32)] * 2
    for row in range(rows):
        total = None
        for a in range(3):
            source = row + a - 1
            if 0 <= source < rows:
                part = jnp.dot(
                    x_ref[source * cols : (source + 1) * cols, :],
                    taps_of(k_ref, a),
                    preferred_element_type=F32,
                )
                total = part if total is None else total + part
        value = joined(total, channels)
        out_ref[row * cols : (row + 1) * cols, :] = value
        if 0 < row < rows - 1:
            sums = with_sums(sums, value)
    return sums


def with_sums(sums, value):
    added = [jnp.sum(v, axis=0, keepdims=True) for v in (value, value * value)]
    return [total + part for total, part in zip(sums, added)]


def edges_kernel(
    rows_fine,
    rows_coarse,
    part_ref,
    inner_ref,
    off_ref,
    on_ref,
    fk_ref,
    ck_ref,
    edges_ref,
    stats_ref,
):
    fine_size = part_ref.shape[0] * 4 // 5
    above, below = above_below(off_ref, on_ref)
    start = 0
    found = []
    for level, (level_ref, k_ref, rows) in enumerate(
        zip(levels(part_ref, fine_size), (fk_ref, ck_ref), (rows_fine, rows_coarse))
    ):
        cols = level_ref.shape[0] // rows
        channels = k_ref.shape[2]
        sums = [inner_ref[2 * level + at : 2 * level + at + 1, :] for at in range(2)]
        for edge, (row, halo, a) in enumerate(((0, above, 0), (rows - 1, below, 2))):
            product = jnp.dot(
                halo[start : start + cols, :], taps_of(k_ref, a), preferred_element_type=F32
            )
            value = level_ref[row * cols : (row + 1) * cols, :] + joined(product, channels)
            to = 2 * start + edge * cols
            edges_ref[to : to + cols, :] = value
            sums = with_sums(sums, value)
        found += sums
        start += cols
    gather, _, own_block = lane_blocks(channels)
    stats_ref[...] = jnp.broadcast_to(packed_sums(found, gather, own_block), stats_ref.shape)


def conv_rows(part_ref, edges_ref, level, row, rows):
    wide = edges_ref.shape[0] // 3
    cols = wide // (level + 1)
    if 0 < row < rows - 1:
        return part_ref[row * cols : (row + 1) * cols, :]
    at = 2 * level * wide + (cols if row else 0)
    return edges_ref[at : at + cols, :]


def over_tiles(all_ref, count):
    return jnp.sum(all_ref[...].astype(F32).reshape(-1, count, all_ref.shape[1]), axis=0)


def stats_sums(stats_ref, channels):
    _, spread, own_block = lane_blocks(channels)
    total = jnp.sum(stats_ref[...], axis=0, keepdims=True)
    return over_group(jnp.where(own_block, total, 0.0), spread)


def packed_sums(rows, gather, own_block):
    groups = over_group(jnp.concatenate(rows, axis=0), gather)
    return jnp.sum(jnp.where(own_block, groups, 0.0), axis=0, keepdims=True)


def lane_blocks(channels):
    per_group = channels // GROUPS
    row = lax.broadcasted_iota(jnp.int32, (channels, channels), 0)
    col = lax.broadcasted_iota(jnp.int32, (channels, channels), 1)
    block_row = lax.broadcasted_iota(jnp.int32, (per_group, channels), 0)
    block_col = lax.broadcasted_iota(jnp.int32, (per_group, channels), 1)
    gather = (row // per_group == lax.rem(col, GROUPS)).astype(F32)
    back = (lax.rem(row, GROUPS) == col // per_group).astype(F32)
    return gather, back, block_col // GROUPS == block_row


def three_parts(values):
    high = values.astype(BF16).astype(F32)
    middle = (values - high).astype(BF16).astype(F32)
    return [high, middle, values - high - middle]


def over_group(rows, members):
    return jnp.dot(rows, members, precision=lax.Precision.HIGHEST, preferred_element_type=F32)


def norm_terms(sums, level, number):
    mean = sums[2 * level : 2 * level + 1, :] / number
    variance = sums[2 * level + 1 : 2 * level + 2, :] / number - mean * mean
    return mean, lax.rsqrt(variance + epsilon)


def loss_kernel(
    rows_fine,
    numbers,
    conv_ref,
    edges_ref,
    stats_ref,
    vectors_ref,
    class_ref,
    labels_ref,
    dpre_ref,
    head_ref,
    wide_ref,
    sum_ref,
):
    fine_size = conv_ref.shape[0] * 4 // 5
    fconv_ref, cconv_ref = levels(conv_ref, fine_size)
    fdpre_ref, cdpre_ref = levels(dpre_ref, fine_size)
    channels = conv_ref.shape[1]
    cols = fconv_ref.shape[0] // rows_fine
    half = cols // 2
    classes = class_ref.shape[0]
    sums = stats_sums(stats_ref, channels)
    fmean, fscale = norm_terms(sums, 0, numbers[0])
    cmean, cscale = norm_terms(sums, 1, numbers[1])
    weights = class_ref[...]
    bias = vectors_ref[8 : 8 + classes, 0:1]
    fgain, foffset = vectors_ref[0:1, :], vectors_ref[1:2, :]
    cgain, coffset = vectors_ref[2:3, :], vectors_ref[3:4, :]
    twice = jnp.concatenate([weights.astype(F32)] * 2, axis=0).astype(BF16)
    rows_sum = [jnp.zeros((1, channels), F32) for _ in range(4)]
    class_sum = jnp.zeros((classes, channels), F32)
    loss_sum = jnp.zeros((1, 2 * cols), F32)
    tissue_sum = jnp.zeros((1, 2 * cols), F32)
    class_id = lax.broadcasted_iota(jnp.int32, (classes, 2 * cols), 0)
    for pair in range(rows_fine // 2):
        cconv = conv_rows(cconv_ref, edges_ref, 1, pair, rows_fine // 2)
        cnormed = (cconv - cmean) * cscale
        cpre = cnormed * cgain + coffset
        cact = jnp.maximum(cpre, 0.0)
        wide_ref[pl.ds(0, half, stride=2), :] = cact
        wide_ref[pl.ds(1, half, stride=2), :] = cact
        up = wide_ref[...]
        up = jnp.concatenate([up, up], axis=0)
        here = slice(2 * pair * cols, 2 * (pair + 1) * cols)
        fconv = [conv_rows(fconv_ref, edges_ref, 0, 2 * pair + at, rows_fine) for at in range(2)]
        normed = (jnp.concatenate(fconv, axis=0) - fmean) * fscale
        pre = normed * fgain + foffset
        merged = (jnp.maximum(pre, 0.0) + up).astype(BF16)
        logits = (
            lax.dot_general(weights, merged, (((1,), (1,)), ((), ())), preferred_element_type=F32)
            + bias
        )
        top = jnp.max(logits, axis=0, keepdims=True)
        lse = top + jnp.log(jnp.sum(jnp.exp(logits - top), axis=0, keepdims=True))
        label = jnp.concatenate(
            [labels_ref[2 * pair : 2 * pair + 1, :], labels_ref[2 * pair + 1 : 2 * pair + 2, :]],
            axis=1,
        )
        tissue = (label >= 0).astype(F32)
        onehot = (label == class_id).astype(F32)
        loss_sum = loss_sum + (lse - jnp.sum(onehot * logits, axis=0, keepdims=True)) * tissue
        tissue_sum = tissue_sum + tissue
        dlogits = (jnp.exp(logits - lse) - onehot) * tissue
        high = dlogits.astype(BF16).astype(F32)
        parts = jnp.concatenate([high, dlogits - high], axis=0).astype(BF16)
        class_part = jnp.dot(parts, merged, preferred_element_type=F32)
        class_sum = class_sum + (class_part[:classes] + class_part[classes:])
        dmerged = lax.dot_general(
            parts, twice, (((0,), (0,)), ((), ())), preferred_element_type=F32
        )
        dpre = jnp.where(pre > 0, dmerged, 0.0)
        fdpre_ref[here, :] = dpre
        rows_sum[0] = rows_sum[0] + jnp.sum(dpre * normed, axis=0, keepdims=True)
        rows_sum[1] = rows_sum[1] + jnp.sum(dpre, axis=0, keepdims=True)
        both = dmerged[:cols] + dmerged[cols:]
        sum_ref[...] = both
        dact = sum_ref[pl.ds(0, half, stride=2), :] + sum_ref[pl.ds(1, half, stride=2), :]
        dpre = jnp.where(cpre > 0, dact, 0.0)
        cdpre_ref[pair * half : (pair + 1) * half, :] = dpre
        rows_sum[2] = rows_sum[2] + jnp.sum(dpre * cnormed, axis=0, keepdims=True)
        rows_sum[3] = rows_sum[3] + jnp.sum(dpre, axis=0, keepdims=True)
    gains = (fgain, fgain, cgain, cgain)
    gather, _, own_block = lane_blocks(channels)
    packed = packed_sums([row * gain for row, gain in zip(rows_sum, gains)], gather, own_block)
    lane = lax.broadcasted_iota(jnp.int32, (1, channels), 1)
    scalars = jnp.zeros((1, channels), F32)
    totals = [jnp.sum(row, axis=1, keepdims=True) for row in (loss_sum, tissue_sum)]
    for at, part in enumerate(three_parts(totals[0]) + three_parts(totals[1])):
        scalars = jnp.where(lane == at, part, scalars)
    head = rows_sum + [class_sum] + three_parts(packed) + [scalars]
    head = jnp.concatenate(head, axis=0).astype(BF16)
    for tile in range(head_ref.shape[0] // 16):
        head_ref[16 * tile : 16 * tile + 16, :] = head


def weights_kernel(
    rows_fine,
    numbers,
    all_conv_ref,
    edges_ref,
    all_dpre_ref,
    stats_ref,
    back_ref,
    vectors_ref,
    all_turn_ref,
    off_ref,
    on_ref,
    keep_ref,
    send_ref,
    head_ref,
    fd_ref,
    cd_ref,
    wide_ref,
):
    fine_size = fd_ref.shape[0]
    fconv_ref, cconv_ref = levels(all_conv_ref, fine_size)
    fdpre_ref, cdpre_ref = levels(all_dpre_ref, fine_size)
    fturn_ref, cturn_ref = levels(all_turn_ref, fine_size, 1)
    channels = all_conv_ref.shape[1]
    sums = stats_sums(stats_ref, channels)
    back = over_tiles(back_ref, 16)
    lane = lax.broadcasted_iota(jnp.int32, (1, channels), 1)
    loss_all, tissue_all = [
        back[15:16, at : at + 1] + back[15:16, at + 1 : at + 2] + back[15:16, at + 2 : at + 3]
        for at in (0, 3)
    ]
    counts = jnp.where(lane == 0, loss_all, jnp.where(lane == 1, tissue_all, 0.0))
    head_ref[...] = jnp.concatenate([back[0:12, :], counts, jnp.zeros((3, channels), F32)], axis=0)
    _, spread, own_block = lane_blocks(channels)
    packed = back[12:13, :] + back[13:14, :] + back[14:15, :]
    back = over_group(jnp.where(own_block, packed, 0.0), spread)
    kept = keep_ref.shape[0] // 16
    order = channel_order(off_ref.shape[1])
    above, below = [turn(order, rows) for rows in above_below(off_ref, on_ref)]
    start = 0
    for level, (conv_ref, dpre_ref, turn_ref, d_ref, rows) in enumerate(
        (
            (fconv_ref, fdpre_ref, fturn_ref, fd_ref, rows_fine),
            (cconv_ref, cdpre_ref, cturn_ref, cd_ref, rows_fine // 2),
        )
    ):
        size = conv_ref.shape[0]
        cols = size // rows
        mean, scale = norm_terms(sums, level, numbers[level])
        gain = vectors_ref[2 * level : 2 * level + 1, :]
        means = back[2 * level : 2 * level + 2, :] / numbers[level]
        with_normed, plain = means[0:1, :], means[1:2, :]
        for row in range(rows):
            here = slice(row * cols, (row + 1) * cols)
            normed = (conv_rows(conv_ref, edges_ref, level, row, rows) - mean) * scale
            dconv = (dpre_ref[here, :] * gain - plain - normed * with_normed) * scale
            d_ref[here, :channels] = moved(dconv, -1).astype(BF16)
            d_ref[here, channels : 2 * channels] = dconv.astype(BF16)
            d_ref[here, 2 * channels :] = moved(dconv, 1).astype(BF16)
        for a in range(3):
            if a == 0:
                product = jnp.dot(
                    turn_ref[:, : size - cols], d_ref[cols:, :], preferred_element_type=F32
                ) + jnp.dot(
                    above[:, start : start + cols], d_ref[:cols, :], preferred_element_type=F32
                )
            elif a == 1:
                product = jnp.dot(turn_ref[...], d_ref[...], preferred_element_type=F32)
            else:
                product = jnp.dot(
                    turn_ref[:, cols:], d_ref[: size - cols, :], preferred_element_type=F32
                ) + jnp.dot(
                    below[:, start : start + cols],
                    d_ref[size - cols :, :],
                    preferred_element_type=F32,
                )
            wide = product.shape[1]
            span = slice(a * wide, (a + 1) * wide)
            for block in range(product.shape[0] // 8):
                piece = product[8 * block : 8 * block + 8, :]
                at = 16 * (block % kept) + 8 * level
                to_ref = keep_ref if block < kept else wide_ref
                to_ref[at : at + 8, span] = piece
        start += cols
    send_ref[...] = wide_ref[...].astype(BF16)


def first_sum_kernel(keep_ref, sent_ref, own_ref, *out_refs):
    size = own_ref.shape[0]
    own_ref[...] = keep_ref[:size, :] + sent_ref[:size, :].astype(F32)
    for at, out_ref in enumerate(out_refs):
        here = slice((at + 1) * size, (at + 2) * size)
        out_ref[...] = (keep_ref[here, :] + sent_ref[here, :].astype(F32)).astype(BF16)


def next_sum_kernel(keep_ref, one_ref, two_ref, three_ref, own_ref, *out_refs):
    size = own_ref.shape[0]
    for at, out_ref in enumerate((own_ref, *out_refs)):
        here = slice(at * size, (at + 1) * size)
        out_ref[...] = (
            (keep_ref[here, :] + one_ref[here, :].astype(F32))
            + (two_ref[here, :].astype(F32) + three_ref[here, :].astype(F32))
        ).astype(out_ref.dtype)


def to_message(grads, head, out_ref):
    wide, channels = grads.shape[1], head.shape[1]
    out_ref[:, :wide] = grads.astype(BF16)
    for at, part in enumerate(three_parts(head)):
        out_ref[:, wide + at * channels : wide + (at + 1) * channels] = part.astype(BF16)


def from_message(ref, wide):
    values = ref[...].astype(F32)
    channels = (values.shape[1] - wide) // 3
    high, middle, low = [
        values[:, wide + at * channels : wide + (at + 1) * channels] for at in range(3)
    ]
    return values[:, :wide], high + middle + low


def last_tile_kernel(keep_ref, one_ref, two_ref, three_ref, head_ref, out_ref):
    grads = (keep_ref[...] + one_ref[...].astype(F32)) + (
        two_ref[...].astype(F32) + three_ref[...].astype(F32)
    )
    to_message(grads, head_ref[...], out_ref)


def pair_kernel(wide, own_ref, other_ref, out_ref):
    grads, head = from_message(own_ref, wide)
    other_grads, other_head = from_message(other_ref, wide)
    to_message(grads + other_grads, head + other_head, out_ref)


def final_kernel(own_ref, one_ref, two_ref, three_ref, loss_ref, head_ref, grads_ref):
    rows, channels = head_ref.shape
    wide = own_ref.shape[1] - 3 * channels
    parts = [from_message(ref, wide) for ref in (own_ref, one_ref, two_ref, three_ref)]
    whole, head = [(own + two) + (one + three) for own, one, two, three in zip(*parts)]
    total = head[rows : rows + 1, 1:2]
    loss_ref[...] = head[rows : rows + 1, 0:1] / total
    head_ref[...] = head[:rows, :] / total
    taps = wide // channels
    for level in range(2):
        for tap in range(taps):
            grads_ref[pl.ds(2 * tap + level, 8, stride=2 * taps), :] = (
                whole[8 * level : 8 * level + 8, tap * channels : (tap + 1) * channels] / total
            )


def swaps(firsts):
    return [pair for i in firsts for pair in ((i, i + 1), (i + 1, i))]


def core_pairs():
    return [(i, i ^ 1) for i in range(32)]


def x_pairs(step):
    return [(i, (i // 8 + step) % 4 * 8 + i % 8) for i in range(32)]


def z_pairs(step):
    return [(i, i // 8 * 8 + (i // 2 + step) % 4 * 2 + i % 2) for i in range(32)]


def per_device(
    fine_level,
    coarse_level,
    fine_kernel,
    coarse_kernel,
    fine_gain,
    fine_offset,
    coarse_gain,
    coarse_offset,
    class_kernel,
    class_offset,
    tissue_labels,
):
    tiles = lax.axis_size("tile")
    in_channels, _, channels = fine_kernel.shape
    _, height, width, _ = fine_level.shape
    classes = class_kernel.shape[0]
    numbers = (
        float(height * tiles * width * (channels // GROUPS)),
        float(height * tiles * width * (channels // GROUPS) // 4),
    )
    fine_size, coarse_size = height * width, height * width // 4
    pixels = fine_size + coarse_size
    fine = fine_level.reshape(fine_size, in_channels)
    coarse = coarse_level.reshape(coarse_size, in_channels)
    fk = fine_kernel.transpose(1, 0, 2)
    ck = coarse_kernel.transpose(1, 0, 2)
    labels = tissue_labels[0]
    vectors = [fine_gain, fine_offset, coarse_gain, coarse_offset]
    vectors = [vector[None, :] for vector in vectors]

    with jax.named_scope("halo"):
        odd = (lax.axis_index("tile") & 1).astype(jnp.uint32)

        def edge_rows(last):
            parts = []
            for rows, size in ((fine, width), (coarse, width // 2)):
                start = last * jnp.uint32(rows.shape[0] - size)
                parts.append(lax.dynamic_slice(rows, (start, jnp.uint32(0)), (size, in_channels)))
            return jnp.concatenate(parts)

        off, on = edge_rows(odd), edge_rows(1 - odd)
        off = lax.ppermute(off, "tile", swaps(range(1, tiles - 1, 2)))
        on = lax.ppermute(on, "tile", swaps(range(0, tiles, 2)))
    with jax.named_scope("forward"):
        whole = pl.BlockSpec(memory_space=pltpu.VMEM)
        conv, turned, vectors, inner = call(
            functools.partial(interior_kernel, height, height // 2),
            (
                shape(pixels, channels),
                shape(in_channels, pixels, dtype=BF16),
                shape(8 + classes, channels),
                shape(8, channels),
            ),
            in_specs=[whole] * 8 + [pl.BlockSpec(memory_space=pltpu.SMEM)],
        )(fine, coarse, fk, ck, *vectors, class_offset)
        edges, stats = call(
            functools.partial(edges_kernel, height, height // 2),
            (shape(3 * width, channels), shape(tiles, channels)),
        )(conv, inner, off, on, fk, ck)
    with jax.named_scope("forward_sums"):
        stats = lax.all_to_all(stats, "tile", 0, 0, tiled=True)
    with jax.named_scope("loss_and_head"):
        dpre, head = call(
            functools.partial(loss_kernel, height, numbers),
            (shape(pixels, channels), shape(16 * tiles, channels, dtype=BF16)),
            (pltpu.VMEM((width, channels), F32), pltpu.VMEM((width, channels), F32)),
        )(conv, edges, stats, vectors, class_kernel, labels)
    with jax.named_scope("backward_sums"):
        head = lax.all_to_all(head, "tile", 0, 0, tiled=True)
    with jax.named_scope("weight_grads"):
        wide = 9 * channels
        keep, send, head = call(
            functools.partial(weights_kernel, height, numbers),
            (
                shape(in_channels, wide),
                shape(in_channels, wide, dtype=BF16),
                shape(16, channels),
            ),
            (
                pltpu.VMEM((fine_size, 3 * channels), BF16),
                pltpu.VMEM((coarse_size, 3 * channels), BF16),
                pltpu.VMEM((in_channels, wide), F32),
            ),
        )(conv, edges, dpre, stats, head, vectors, turned, off, on)
    with jax.named_scope("over_tiles"):
        sent = lax.ppermute(send, "tile", core_pairs())
        size = in_channels // 4
        parts = call(
            first_sum_kernel, (shape(size, wide),) + (shape(size, wide, dtype=BF16),) * 3
        )(keep, sent)
        got = [lax.ppermute(parts[step], "tile", x_pairs(step)) for step in (2, 1, 3)]
        size = size // 4
        parts = call(
            next_sum_kernel, (shape(size, wide),) + (shape(size, wide, dtype=BF16),) * 3
        )(parts[0], *got)
        got = [lax.ppermute(parts[step], "tile", z_pairs(step)) for step in (1, 2, 3)]
        message = shape(size, wide + 3 * channels, dtype=BF16)
        own = call(last_tile_kernel, message)(parts[0], *got, head)
    with jax.named_scope("over_slides"):
        slides = lax.axis_size("slide")
        other = lax.ppermute(own, "slide", [(i, i ^ 1) for i in range(slides)])
        own = call(functools.partial(pair_kernel, wide), message)(own, other)
        got = [
            lax.ppermute(own, "slide", [(i, (i + 2 * step) % slides) for i in range(slides)])
            for step in (1, 2, 3)
        ]
        loss, head_grads, grads = call(
            final_kernel,
            (shape(1, 1), shape(4 + classes, channels), shape(in_channels // tiles * 18, channels)),
        )(own, *got)
    conv_grads = grads.reshape(in_channels // tiles, 9, 2, channels).transpose(0, 2, 1, 3)
    return (loss.reshape(()), head_grads, conv_grads)


def solution(mesh):
    return jax.shard_map(
        per_device,
        mesh=mesh,
        in_specs=(
            P("slide", "tile", None, None),
            P("slide", "tile", None, None),
            P(),
            P(),
            P(),
            P(),
            P(),
            P(),
            P(),
            P(),
            P("slide", "tile", None),
        ),
        out_specs=(P(), P(), P("tile", None, None, None)),
        check_vma=False,
    )
```
